256 devices in a mesh: lon: 16 (over y_hi, z), lat: 16 (over x, y_lo, core).
Axes of the slice: x: 4, y: 4 (y_hi: 2, y_lo: 2; y = y_hi * 2 + y_lo), z: 8, core: 2. Of those that a mesh axis runs over, the one named last changes fastest.
Arguments:
- u_velocity: float32 [12, 1536, 2048], P(None, 'lat', 'lon'), may hold values from -6 to 6
- v_velocity: float32 [12, 1536, 2048], P(None, 'lat', 'lon'), may hold values from -6 to 6
- density: float32 [12, 1536, 2048], P(None, 'lat', 'lon'), may hold values from -6 to 6
- surface: float32 [1536, 2048], P('lat', 'lon'), may hold values from -4 to 4
- land_mask: int32 [12, 1536, 2048], P(None, 'lat', 'lon'), may hold values from 0 to 1, as said below
- bottom: int32 [1536, 2048], P('lat', 'lon'), may hold values from 0 to 12
Outputs:
- u_final: float32 [12, 1536, 2048], P(None, 'lat', 'lon')
- v_final: float32 [12, 1536, 2048], P(None, 'lat', 'lon')
- surface_final: float32 [1536, 2048], P('lat', 'lon')
The draws below stay inside these ranges and needn't reach their ends.
Inputs may be any that keep to these rules, and one draw needn't show every extreme that they name: land_mask is 1 only at levels above the column's bottom; in an ocean column every level from its first ocean level (0, 1 or 2) down to bottom - 1 is 1.
All inputs are finite; a program needn't handle non-finite values.
Results may differ from the reference program's by a relative error of at most 0.0003.
Values sent between devices are 32-bit elements; how exact they have to be, the bound alone decides.
No kernel may reach another device: no remote copies, remote signals or barrier semaphores. Data moves between devices by JAX's collectives and lax.ppermute only.
A program may use at most 64 MiB of HBM per device.

```python
import math
import jax
import jax.numpy as jnp
from jax import lax

LEVELS = 12
SUBSTEPS = 8
STEPS = 2
NI = 2048
NJ = 1536


def column_draw(key):
    first = jax.random.fold_in(key, 11)
    second = jax.random.fold_in(key, 12)
    drawn = jax.random.randint(first, (NJ, NI), 0, LEVELS + 16)
    floor_level = jnp.clip(drawn - 8, 0, LEVELS)
    ceiling_raw = jax.random.randint(second, (NJ, NI), -6, 3)
    ceiling = jnp.maximum(ceiling_raw, 0)
    return (floor_level, ceiling)


def draw_bottom(key, part):
    floor_level, ceiling = column_draw(key)
    return floor_level.astype(jnp.int32)


def draw_land_mask(key, part):
    floor_level, ceiling = column_draw(key)
    level_ids = jnp.arange(LEVELS, dtype=jnp.int32)[:, None, None]
    opened = (level_ids < floor_level[None]) & (level_ids >= ceiling[None])
    return opened.astype(jnp.int32)


def block_levels(key, dims, shards, least, largest):
    def one(axis_at, parts):
        draws = jax.random.uniform(jax.random.fold_in(jax.random.fold_in(key, 6), axis_at), (parts,), jnp.float32, least / len(shards), largest / len(shards))
        return jnp.repeat(jnp.exp(draws), dims[axis_at] // parts).reshape((-1,) + (1,) * (len(dims) - axis_at - 1))

    gain = one(*shards[0])
    for cut in shards[1:]:
        gain = gain * one(*cut)
    return gain


def noise(key, shape, spread, reach, pieces=(), held_as=jnp.bfloat16):
    array = spread * jax.random.normal(key, shape, jnp.float32)
    if pieces:
        array = array * block_levels(key, shape, pieces, -0.22, 0.18)
    return jnp.clip(array, -reach, reach).astype(held_as)


def setup_inputs(seed: int = 0) -> dict:
    streams_of = jax.random.split(jax.random.key(seed), 7)
    u_velocity = noise(streams_of[0], (LEVELS, NJ, NI), 1.0, 6.0, ((1, 16), (2, 16)), jnp.float32)
    v_velocity = noise(streams_of[1], (LEVELS, NJ, NI), 1.0, 6.0, ((1, 16), (2, 16)), jnp.float32)
    density = noise(streams_of[2], (LEVELS, NJ, NI), 1.0, 6.0, ((1, 16), (2, 16)), jnp.float32)
    surface = noise(streams_of[3], (NJ, NI), 0.5, 4.0, ((0, 16), (1, 16)), jnp.float32)
    land_mask = draw_land_mask(jax.random.fold_in(streams_of[6], 71), 0)
    bottom = draw_bottom(jax.random.fold_in(streams_of[6], 71), 0)
    return {"u_velocity": u_velocity, "v_velocity": v_velocity, "density": density, "surface": surface, "land_mask": land_mask, "bottom": bottom}


gravity = 1.0
buoyancy = 1.0
viscosity = 0.05
friction = 0.1
coriolis = 0.25
substep_time = 0.4


def eastward(field):
    return jnp.roll(field, -1, axis=-1)


def westward(field):
    return jnp.roll(field, 1, axis=-1)


def southward(field):
    edge = jnp.zeros_like(field[..., :1, :])
    return jnp.concatenate([edge, field[..., :-1, :]], axis=-2)


def northward(field, kind):
    below = field[..., -2:-1, :]
    flipped = jnp.flip(below, -1)
    if kind == "t":
        ghost = flipped
    elif kind == "v":
        ghost = -flipped
    else:
        ghost = -jnp.roll(flipped, -1, axis=-1)
    return jnp.concatenate([field[..., 1:, :], ghost], axis=-2)


def reference(u_velocity, v_velocity, density, surface, land_mask, bottom):
    lat_cells = bottom.shape[0]
    layer = 1.0 / LEVELS
    row_ids = jnp.arange(lat_cells).astype(jnp.float32)
    spin_centre = coriolis * jnp.sin(math.pi * ((row_ids + 0.5) / lat_cells - 0.5))[:, None]
    spin_face = coriolis * jnp.sin(math.pi * ((row_ids + 1.0) / lat_cells - 0.5))[:, None]
    level_ids = jnp.arange(LEVELS, dtype=jnp.int32)[:, None, None]
    floor_east = eastward(bottom)
    floor_north = northward(bottom, "t")
    ocean = land_mask.astype(jnp.float32)
    u_mask = ocean * (level_ids < floor_east).astype(jnp.float32)
    v_mask = ocean * (level_ids < floor_north).astype(jnp.float32)
    sea_cells = (bottom > 0).astype(jnp.float32)
    u_wet = jnp.max(u_mask, axis=0)
    v_wet = jnp.max(v_mask, axis=0)
    u_depth = layer * jnp.sum(u_mask, axis=0)
    v_depth = layer * jnp.sum(v_mask, axis=0)
    step_time = SUBSTEPS * substep_time
    drag = 1.0 / (1.0 + step_time * friction)
    u_drag = jnp.where(level_ids == jnp.minimum(bottom, floor_east) - 1, drag, 1.0).astype(jnp.float32)
    v_drag = jnp.where(level_ids == jnp.minimum(bottom, floor_north) - 1, drag, 1.0).astype(jnp.float32)
    weighted = ocean * density
    pressure = buoyancy * layer * (jnp.cumsum(weighted, axis=0) - 0.5 * weighted)
    grad_u = eastward(pressure) - pressure
    grad_v = northward(pressure, "t") - pressure
    u_now = u_velocity * u_mask
    v_now = v_velocity * v_mask
    height = surface * sea_cells
    for step in range(STEPS):
        lap_u = eastward(u_now) + westward(u_now) + northward(u_now, "u") + southward(u_now) - 4.0 * u_now
        lap_v = eastward(v_now) + westward(v_now) + northward(v_now, "v") + southward(v_now) - 4.0 * v_now
        v_at_u = 0.25 * (v_now + eastward(v_now) + southward(v_now) + southward(eastward(v_now)))
        north_u = northward(u_now, "u")
        u_at_v = 0.25 * (u_now + westward(u_now) + north_u + westward(north_u))
        tend_u = u_mask * (-grad_u + spin_centre * v_at_u + viscosity * lap_u)
        tend_v = v_mask * (-grad_v - spin_face * u_at_v + viscosity * lap_v)
        force_u = layer * jnp.sum(tend_u, axis=0)
        force_v = layer * jnp.sum(tend_v, axis=0)
        flow_u = layer * jnp.sum(u_now, axis=0)
        flow_v = layer * jnp.sum(v_now, axis=0)

        def substep(turn, carry):
            level, east_flow, north_flow, total_u, total_v = carry
            level = sea_cells * (level - substep_time * (east_flow - westward(east_flow) + north_flow - southward(north_flow)))
            flow_at_u = 0.25 * (north_flow + eastward(north_flow) + southward(north_flow) + southward(eastward(north_flow)))
            upper_flow = northward(east_flow, "u")
            flow_at_v = 0.25 * (east_flow + westward(east_flow) + upper_flow + westward(upper_flow))
            next_u = u_wet * (east_flow + substep_time * (-gravity * u_depth * (eastward(level) - level) + spin_centre * flow_at_u + force_u))
            next_v = v_wet * (north_flow + substep_time * (-gravity * v_depth * (northward(level, "t") - level) - spin_face * flow_at_v + force_v))
            return (level, next_u, next_v, total_u + next_u, total_v + next_v)

        start = (height, flow_u, flow_v, jnp.zeros_like(flow_u), jnp.zeros_like(flow_v))
        height, flow_u, flow_v, total_u, total_v = lax.fori_loop(0, SUBSTEPS, substep, start)
        mean_u = total_u / SUBSTEPS
        mean_v = total_v / SUBSTEPS
        new_u = u_drag * (u_now + step_time * tend_u)
        new_v = v_drag * (v_now + step_time * tend_v)
        u_now = u_mask * (new_u + (mean_u - layer * jnp.sum(new_u, axis=0)) / jnp.maximum(u_depth, layer))
        v_now = v_mask * (new_v + (mean_v - layer * jnp.sum(new_v, axis=0)) / jnp.maximum(v_depth, layer))
    return u_now, v_now, height
```

```python
import math

import jax
import jax.numpy as jnp
from jax import lax
from jax.experimental import pallas as pl
from jax.experimental.pallas import tpu as pltpu
from jax.sharding import PartitionSpec as P

SUBSTEPS = 8
STEPS = 2
LEVELS = 12
ROWS = 96
LANES = 128
HALO = 16
FOLD = 18

PLANES = 3 * LEVELS + 3
BOTTOM, FIRST, SURFACE = 36, 37, 38
PACKS = -(-PLANES // 8)
SENT = PLANES + 2 * PACKS

PAD = 8
EXT = 136
TALL = PAD + EXT + PAD
OWN = HALO
GHOST_A, PATCH, GHOST_B = OWN + ROWS, OWN + ROWS + 1, OWN + ROWS + 1 + FOLD
CHUNKS = ((0, 32), (32, 32), (64, 32), (96, 40))

viscosity = 0.05
friction = 0.1
coriolis = 0.25
substep_time = 0.4
layer = 1.0 / LEVELS
step_time = SUBSTEPS * substep_time
drag = 1.0 / (1.0 + step_time * friction)

VMEM_LIMIT = 56 * 1024 * 1024


def lanes_of(shape):
    return lax.broadcasted_iota(jnp.int32, shape, len(shape) - 1)


def prepare(u_ref, v_ref, d_ref, s_ref, m_ref, b_ref, own_ref, a_ref, c_ref):
    lane = lanes_of((ROWS, LANES))
    row = lax.broadcasted_iota(jnp.int32, (ROWS, LANES), 0)
    bottom = b_ref[...].astype(jnp.float32)
    ocean = [m_ref[k].astype(jnp.float32) for k in range(LEVELS)]
    first = bottom - sum(ocean)
    east = jnp.where(lane == LANES - 1, 12.0, pltpu.roll(bottom, LANES - 1, 1))
    north = jnp.where(row == ROWS - 1, 12.0, pltpu.roll(bottom, ROWS - 1, 0))
    running = jnp.zeros_like(bottom)
    for k in range(LEVELS):
        weighted = ocean[k] * d_ref[k]
        running = running + weighted
        own_ref[k] = jnp.where(east > k, ocean[k] * u_ref[k], 0.0)
        own_ref[LEVELS + k] = jnp.where(north > k, ocean[k] * v_ref[k], 0.0)
        own_ref[2 * LEVELS + k] = layer * (running - 0.5 * weighted)
    own_ref[BOTTOM] = bottom
    own_ref[FIRST] = first
    own_ref[SURFACE] = jnp.where(bottom > 0.0, s_ref[...], 0.0)
    even = lax.rem(lax.axis_index("lon"), 2) == 0
    for pack in range(PACKS):
        to_east = jnp.zeros((ROWS, LANES), jnp.float32)
        to_west = jnp.zeros((ROWS, LANES), jnp.float32)
        for slot in range(min(8, PLANES - 8 * pack)):
            plane = own_ref[8 * pack + slot]
            here = (lane >= HALO * slot) & (lane < HALO * slot + HALO)
            to_east = jnp.where(here, pltpu.roll(plane, (HALO * slot + HALO) % LANES, 1), to_east)
            moved = pltpu.roll(plane, HALO * slot, 1) if slot else plane
            to_west = jnp.where(here, moved, to_west)
        a_ref[pack] = jnp.where(even, to_east, to_west)
        c_ref[pack] = jnp.where(even, to_west, to_east)


def outer_rows(low_own, low_a, low_b, top_own, top_a, top_b, a_ref, c_ref):
    even = lax.rem(lax.axis_index("lat"), 2) == 0
    for p in range(SENT):
        if p < PLANES:
            low, top = low_own[p], top_own[p]
        elif p < PLANES + PACKS:
            low, top = low_a[p - PLANES], top_a[p - PLANES]
        else:
            low, top = low_b[p - PLANES - PACKS], top_b[p - PLANES - PACKS]
        a_ref[pl.ds(p * HALO, HALO), :] = jnp.where(even, top[24 - HALO :], low[:HALO])
        c_ref[pl.ds(p * FOLD, FOLD), :] = jnp.where(even, low[:FOLD], top[24 - FOLD :])


def eastward(t0, t1):
    lane = lanes_of(t0.shape)
    r0, r1 = pltpu.roll(t0, LANES - 1, t0.ndim - 1), pltpu.roll(t1, LANES - 1, t0.ndim - 1)
    edge = lane == LANES - 1
    return jnp.where(edge, r1, r0), jnp.where(edge, r0, r1)


def westward(t0, t1):
    lane = lanes_of(t0.shape)
    r0, r1 = pltpu.roll(t0, 1, t0.ndim - 1), pltpu.roll(t1, 1, t0.ndim - 1)
    edge = lane == 0
    return jnp.where(edge, r1, r0), jnp.where(edge, r0, r1)


def fold_ghosts(ref, top, sign=1.0):
    for t in range(2):
        for ghost, source in ((GHOST_A, PATCH + FOLD - 2), (GHOST_B, OWN + ROWS - 2)):
            kept = ref[t, pl.ds(PAD + ghost, 1), :]
            taken = ref[t, pl.ds(PAD + source, 1), :]
            ref[t, pl.ds(PAD + ghost, 1), :] = jnp.where(top, sign * taken, kept)


def ocean_steps(
    own_ref, ea_ref, eb_ref, na_ref, nb_ref, ft_ref, fv_ref,
    u_out, v_out, h_out,
    u_all, v_all, p_all, u_new, v_new,
    flat, flow_u, flow_v, height,
):
    lat = lax.axis_index("lat")
    even_lat = lax.rem(lat, 2) == 0
    even_lon = lax.rem(lax.axis_index("lon"), 2) == 0
    top = lat == lax.axis_size("lat") - 1
    a_side = jnp.where(even_lon, 0, LANES - HALO)
    b_side = jnp.where(even_lon, LANES - HALO, 0)
    (BED, FROM, UP_U, LO_U, UP_V, C_U, F_U, G_U, C_V, F_V, G_V, SUM_U, SUM_V, NEW_U, NEW_V, SEA) = range(16)

    def place(p):
        if p < LEVELS:
            return u_all.at[p]
        if p < 2 * LEVELS:
            return v_all.at[p - LEVELS]
        if p < 3 * LEVELS:
            return p_all.at[p - 2 * LEVELS]
        return {BOTTOM: flat.at[BED], FIRST: flat.at[FROM], SURFACE: height}[p]

    def side(a, b, p, shape):
        lane = lanes_of(shape)
        slot = HALO * (p % 8)
        from_a = pltpu.roll(a, lax.rem(a_side - slot + LANES, LANES), 1)
        from_b = pltpu.roll(b, lax.rem(b_side - slot + LANES, LANES), 1)
        in_a = (lane >= a_side) & (lane < a_side + HALO)
        in_b = (lane >= b_side) & (lane < b_side + HALO)
        outside = 12.0 if p in (BOTTOM, FIRST) else 0.0
        return jnp.where(in_a, from_a, jnp.where(in_b, from_b, outside))

    def north_rows(p):
        return jnp.where(even_lat, na_ref[pl.ds(p * HALO, HALO), :], nb_ref[pl.ds(p * FOLD, HALO), :])

    def south_rows(p):
        return jnp.where(even_lat, nb_ref[pl.ds(p * FOLD + FOLD - HALO, HALO), :], na_ref[pl.ds(p * HALO, HALO), :])

    for p in range(PLANES):
        ref = place(p)
        beyond = 12.0 if p in (BOTTOM, FIRST) else 0.0
        pa, pb = PLANES + p // 8, PLANES + PACKS + p // 8
        ref[0, pl.ds(PAD, HALO), :] = south_rows(p)
        ref[0, pl.ds(PAD + OWN, ROWS), :] = own_ref[p]
        ref[0, pl.ds(PAD + OWN + ROWS, HALO), :] = north_rows(p)
        ref[1, pl.ds(PAD, HALO), :] = side(south_rows(pa), south_rows(pb), p, (HALO, LANES))
        ref[1, pl.ds(PAD + OWN, ROWS), :] = side(ea_ref[p // 8], eb_ref[p // 8], p, (ROWS, LANES))
        ref[1, pl.ds(PAD + OWN + ROWS, HALO), :] = side(north_rows(pa), north_rows(pb), p, (HALO, LANES))
        for t in range(2):
            ref[t, pl.ds(0, PAD), :] = jnp.full((PAD, LANES), beyond, jnp.float32)
            ref[t, pl.ds(PAD + OWN + ROWS + HALO, 16), :] = jnp.full((16, LANES), beyond, jnp.float32)

    @pl.when(top)
    def _():
        flip_row = lax.broadcasted_iota(jnp.int32, (LANES, LANES), 0)
        flip_lane = lax.broadcasted_iota(jnp.int32, (LANES, LANES), 1)
        flip = (flip_row + flip_lane == LANES - 1).astype(jnp.float32)

        def flipped(x):
            return jnp.dot(x, flip, precision=lax.Precision.HIGHEST, preferred_element_type=jnp.float32)

        for p in range(PLANES):
            ref = place(p)
            pa, pb = PLANES + p // 8, PLANES + PACKS + p // 8
            lane = lanes_of((FOLD, LANES))
            slot = HALO * (p % 8)
            a, b = nb_ref[pl.ds(pa * FOLD, FOLD), :], nb_ref[pl.ds(pb * FOLD, FOLD), :]
            from_a = pltpu.roll(a, lax.rem(b_side - slot + LANES, LANES), 1)
            from_b = pltpu.roll(b, lax.rem(a_side - slot + LANES, LANES), 1)
            in_a = (lane >= b_side) & (lane < b_side + HALO)
            in_b = (lane >= a_side) & (lane < a_side + HALO)
            outside = 12.0 if p in (BOTTOM, FIRST) else 0.0
            beside = jnp.where(in_a, from_a, jnp.where(in_b, from_b, outside))
            t0, t1 = flipped(nb_ref[pl.ds(p * FOLD, FOLD), :]), flipped(beside)
            if p < LEVELS:
                t0, t1 = eastward(t0, t1)
                t0, t1 = -t0, -t1
            ref[0, pl.ds(PAD + PATCH, FOLD), :] = t0
            ref[1, pl.ds(PAD + PATCH, FOLD), :] = t1

    fold_ghosts(flat.at[BED], top)

    for at, n in CHUNKS:
        rows = pl.ds(PAD + at, n)
        up = pl.ds(PAD + at + 1, n)
        bed = [flat[BED, t, rows, :] for t in range(2)]
        start = [flat[FROM, t, rows, :] for t in range(2)]
        bed_east = eastward(*bed)
        start_east = eastward(*start)
        ext_row = lax.broadcasted_iota(jnp.int32, (n, LANES), 0) + at
        mirror = (ext_row >= jnp.where(top, PATCH, EXT)) & (ext_row < PATCH + FOLD)
        for t in range(2):
            up_u = jnp.minimum(bed[t], bed_east[t])
            lo_u = jnp.where(mirror, start_east[t], start[t])
            up_v = jnp.minimum(bed[t], flat[BED, t, up, :])
            count_u = jnp.maximum(up_u - lo_u, 0.0)
            count_v = jnp.maximum(up_v - start[t], 0.0)
            flat[UP_U, t, rows, :] = up_u
            flat[LO_U, t, rows, :] = lo_u
            flat[UP_V, t, rows, :] = up_v
            flat[C_U, t, rows, :] = count_u * (-substep_time * layer)
            flat[C_V, t, rows, :] = count_v * (-substep_time * layer)
            flat[F_U, t, rows, :] = jnp.where(count_u > 0.0, substep_time * ft_ref[rows, :], 0.0)
            flat[F_V, t, rows, :] = jnp.where(count_v > 0.0, -substep_time * fv_ref[rows, :], 0.0)
            flat[SEA, t, rows, :] = jnp.where(bed[t] > 0.0, substep_time, 0.0)

    def mask_at(r, k):
        rows = pl.ds(pl.multiple_of(r * 8, 8) + PAD, 8)
        mu = [(flat[LO_U, t, rows, :] <= k) & (flat[UP_U, t, rows, :] > k) for t in range(2)]
        mv = [(flat[FROM, t, rows, :] <= k) & (flat[UP_V, t, rows, :] > k) for t in range(2)]
        return mu, mv

    def mask_first(r, carry):
        rows = pl.ds(pl.multiple_of(r * 8, 8) + PAD, 8)
        for t in range(2):
            lo_u, up_u = flat[LO_U, t, rows, :], flat[UP_U, t, rows, :]
            lo_v, up_v = flat[FROM, t, rows, :], flat[UP_V, t, rows, :]
            sum_u = jnp.zeros((8, LANES), jnp.float32)
            sum_v = jnp.zeros((8, LANES), jnp.float32)
            for k in range(LEVELS):
                u = jnp.where((lo_u <= k) & (up_u > k), u_all[k, t, rows, :], 0.0)
                v = jnp.where((lo_v <= k) & (up_v > k), v_all[k, t, rows, :], 0.0)
                u_all[k, t, rows, :] = u
                v_all[k, t, rows, :] = v
                sum_u = sum_u + u
                sum_v = sum_v + v
            flow_u[0, t, rows, :] = layer * sum_u
            flow_v[0, t, rows, :] = layer * sum_v
        return carry

    for flow in (flow_u, flow_v):
        for now in range(2):
            for t in range(2):
                flow[now, t, pl.ds(0, PAD), :] = jnp.zeros((PAD, LANES), jnp.float32)
                flow[now, t, pl.ds(PAD + EXT, PAD), :] = jnp.zeros((PAD, LANES), jnp.float32)

    lax.fori_loop(0, EXT // 8, mask_first, 0)

    for step in range(STEPS):
        for k in range(LEVELS):
            fold_ghosts(u_all.at[k], top)
            fold_ghosts(v_all.at[k], top, -1.0)
            if step == 0:
                fold_ghosts(p_all.at[k], top)
        fold_ghosts(flow_u.at[0], top)

        def tendencies(r, carry):
            base = pl.multiple_of(r * 8, 8) + PAD
            rows, up, down = pl.ds(base, 8), pl.ds(base + 1, 8), pl.ds(base - 1, 8)
            ft, fv = ft_ref[rows, :], fv_ref[rows, :]
            lo_u = [flat[LO_U, t, rows, :] for t in range(2)]
            up_u = [flat[UP_U, t, rows, :] for t in range(2)]
            lo_v = [flat[FROM, t, rows, :] for t in range(2)]
            up_v = [flat[UP_V, t, rows, :] for t in range(2)]
            zero = jnp.zeros((8, LANES), jnp.float32)
            force_u, force_v, total_u, total_v = [zero] * 2, [zero] * 2, [zero] * 2, [zero] * 2
            for k in range(LEVELS):
                eu, wu, ru, ev, wv, rv, u0s, v0s = [], [], [], [], [], [], [], []
                for t in range(2):
                    u0, un, us = u_all[k, t, rows, :], u_all[k, t, up, :], u_all[k, t, down, :]
                    v0, vn, vs = v_all[k, t, rows, :], v_all[k, t, up, :], v_all[k, t, down, :]
                    p0, pn = p_all[k, t, rows, :], p_all[k, t, up, :]
                    turn_v = ft * (v0 + vs)
                    turn_u = fv * (u0 + un)
                    a = viscosity * u0
                    c = viscosity * v0
                    eu.append(a - p0 + turn_v)
                    wu.append(a)
                    ru.append(viscosity * (un + us) - 4.0 * a + p0 + turn_v)
                    ev.append(c)
                    wv.append(c - turn_u)
                    rv.append(viscosity * (vn + vs) - 4.0 * c + (p0 - pn) - turn_u)
                    u0s.append(u0)
                    v0s.append(v0)
                eu, wu, ev, wv = eastward(*eu), westward(*wu), eastward(*ev), westward(*wv)
                for t in range(2):
                    tend_u = jnp.where((lo_u[t] <= k) & (up_u[t] > k), eu[t] + wu[t] + ru[t], 0.0)
                    tend_v = jnp.where((lo_v[t] <= k) & (up_v[t] > k), ev[t] + wv[t] + rv[t], 0.0)
                    force_u[t] = force_u[t] + tend_u
                    force_v[t] = force_v[t] + tend_v
                    new_u = u0s[t] + step_time * tend_u
                    new_v = v0s[t] + step_time * tend_v
                    new_u = jnp.where(up_u[t] == k + 1, drag * new_u, new_u)
                    new_v = jnp.where(up_v[t] == k + 1, drag * new_v, new_v)
                    total_u[t] = total_u[t] + new_u
                    total_v[t] = total_v[t] + new_v
                    u_new[k, t, rows, :] = new_u
                    v_new[k, t, rows, :] = new_v
            for t in range(2):
                flat[G_U, t, rows, :] = (substep_time * layer) * force_u[t]
                flat[G_V, t, rows, :] = (substep_time * layer) * force_v[t]
                flat[NEW_U, t, rows, :] = layer * total_u[t]
                flat[NEW_V, t, rows, :] = layer * total_v[t]
                flat[SUM_U, t, rows, :] = zero
                flat[SUM_V, t, rows, :] = zero
            return carry

        lax.fori_loop(0, EXT // 8, tendencies, 0)

        def substep(now, later):
            for at, n in CHUNKS:
                rows, down = pl.ds(PAD + at, n), pl.ds(PAD + at - 1, n)
                u = [flow_u[now, t, rows, :] for t in range(2)]
                uw = westward(*u)
                for t in range(2):
                    spread = u[t] - uw[t] + flow_v[now, t, rows, :] - flow_v[now, t, down, :]
                    height[t, rows, :] = height[t, rows, :] - flat[SEA, t, rows, :] * spread
            fold_ghosts(height, top)
            for at, n in CHUNKS:
                rows, up, down = pl.ds(PAD + at, n), pl.ds(PAD + at + 1, n), pl.ds(PAD + at - 1, n)
                h = [height[t, rows, :] for t in range(2)]
                he = eastward(*h)
                qv = [flow_v[now, t, rows, :] + flow_v[now, t, down, :] for t in range(2)]
                qve = eastward(*qv)
                qu = [flow_u[now, t, rows, :] + flow_u[now, t, up, :] for t in range(2)]
                quw = westward(*qu)
                for t in range(2):
                    next_u = (
                        flow_u[now, t, rows, :]
                        + flat[C_U, t, rows, :] * (he[t] - h[t])
                        + flat[F_U, t, rows, :] * (qv[t] + qve[t])
                        + flat[G_U, t, rows, :]
                    )
                    next_v = (
                        flow_v[now, t, rows, :]
                        + flat[C_V, t, rows, :] * (height[t, up, :] - h[t])
                        + flat[F_V, t, rows, :] * (qu[t] + quw[t])
                        + flat[G_V, t, rows, :]
                    )
                    flow_u[later, t, rows, :] = next_u
                    flow_v[later, t, rows, :] = next_v
                    flat[SUM_U, t, rows, :] = flat[SUM_U, t, rows, :] + next_u
                    flat[SUM_V, t, rows, :] = flat[SUM_V, t, rows, :] + next_v
            fold_ghosts(flow_u.at[later], top)

        def two_substeps(turn, carry):
            substep(0, 1)
            substep(1, 0)
            return carry

        lax.fori_loop(0, SUBSTEPS // 2, two_substeps, 0)

        last = step == STEPS - 1

        def correct(r, carry):
            base = pl.multiple_of(r * 8, 8) + PAD
            rows = pl.ds(base, 8)
            for t in range(1 if last else 2):
                lo_u, up_u = flat[LO_U, t, rows, :], flat[UP_U, t, rows, :]
                lo_v, up_v = flat[FROM, t, rows, :], flat[UP_V, t, rows, :]
                mean_u = flat[SUM_U, t, rows, :] / SUBSTEPS
                mean_v = flat[SUM_V, t, rows, :] / SUBSTEPS
                depth_u = layer * jnp.maximum(up_u - lo_u, 1.0)
                depth_v = layer * jnp.maximum(up_v - lo_v, 1.0)
                add_u = (mean_u - flat[NEW_U, t, rows, :]) / depth_u
                add_v = (mean_v - flat[NEW_V, t, rows, :]) / depth_v
                for k in range(LEVELS):
                    u = jnp.where((lo_u <= k) & (up_u > k), u_new[k, t, rows, :] + add_u, 0.0)
                    v = jnp.where((lo_v <= k) & (up_v > k), v_new[k, t, rows, :] + add_v, 0.0)
                    if last:
                        out = pl.ds(pl.multiple_of(r * 8 - OWN, 8), 8)
                        u_out[k, out, :] = u
                        v_out[k, out, :] = v
                    else:
                        u_all[k, t, rows, :] = u
                        v_all[k, t, rows, :] = v
                if not last:
                    flow_u[0, t, rows, :] = mean_u
                    flow_v[0, t, rows, :] = mean_v
            return carry

        if last:
            lax.fori_loop(OWN // 8, (OWN + ROWS) // 8, correct, 0)
        else:
            lax.fori_loop(0, EXT // 8, correct, 0)

    h_out[...] = height[0, pl.ds(PAD + OWN, ROWS), :]


def lon_swaps():
    count = lax.axis_size("lon")
    first = [(i, i ^ 1) for i in range(count)]
    second = [(i, (((i + 1) % count) ^ 1) - 1) for i in range(count)]
    return first, [(i, j % count) for i, j in second]


def lat_swaps():
    lats, lons = lax.axis_size("lat"), lax.axis_size("lon")
    first, second = [], []
    for lat in range(lats):
        for lon in range(lons):
            first.append((lon * lats + lat, lon * lats + (lat ^ 1)))
            if lat == lats - 1:
                second.append((lon * lats + lat, (lons - 1 - lon) * lats + lat))
            elif lat:
                second.append((lon * lats + lat, lon * lats + ((lat + 1) ^ 1) - 1))
    return first, second


def turning(lat):
    lats = lax.axis_size("lat")
    ext = jnp.arange(TALL, dtype=jnp.int32) - PAD
    mirror = (lat == lats - 1) & (ext >= PATCH)
    row = jnp.where(mirror, lats * ROWS - FOLD + ext - PATCH, lat * ROWS + ext - OWN).astype(jnp.float32)
    sign = jnp.where(mirror, -0.25 * coriolis, 0.25 * coriolis)
    cells = lats * ROWS
    centre = sign * jnp.sin(math.pi * ((row + 0.5) / cells - 0.5))
    face = sign * jnp.sin(math.pi * ((row + 1.0) / cells - 0.5))
    wide = (TALL, LANES)
    return jnp.broadcast_to(centre[:, None], wide), jnp.broadcast_to(face[:, None], wide)


def whole(*shape):
    return pl.BlockSpec(shape, lambda *_: (0,) * len(shape))


def shards(u_velocity, v_velocity, density, surface, land_mask, bottom):
    f32 = jnp.float32
    params = pltpu.CompilerParams(vmem_limit_bytes=VMEM_LIMIT)
    level_block = (LEVELS, ROWS, LANES)
    own, pack_a, pack_b = pl.pallas_call(
        prepare,
        out_shape=(
            jax.ShapeDtypeStruct((PLANES, ROWS, LANES), f32),
            jax.ShapeDtypeStruct((PACKS, ROWS, LANES), f32),
            jax.ShapeDtypeStruct((PACKS, ROWS, LANES), f32),
        ),
        compiler_params=params,
    )(u_velocity, v_velocity, density, surface, land_mask, bottom)
    lon_first, lon_second = lon_swaps()
    east_a = lax.ppermute(pack_a, "lon", lon_first)
    east_b = lax.ppermute(pack_b, "lon", lon_second)

    low = lambda planes: pl.BlockSpec((planes, 24, LANES), lambda i: (0, 0, 0))
    high = lambda planes: pl.BlockSpec((planes, 24, LANES), lambda i: (0, ROWS // 24 - 1, 0))
    rows_a, rows_b = pl.pallas_call(
        outer_rows,
        grid=(1,),
        in_specs=[low(PLANES), low(PACKS), low(PACKS), high(PLANES), high(PACKS), high(PACKS)],
        out_specs=(whole(SENT * HALO, LANES), whole(888, LANES)),
        out_shape=(
            jax.ShapeDtypeStruct((SENT * HALO, LANES), f32),
            jax.ShapeDtypeStruct((888, LANES), f32),
        ),
        compiler_params=params,
    )(own, east_a, east_b, own, east_a, east_b)
    lat_first, lat_second = lat_swaps()
    north_a = lax.ppermute(rows_a, ("lon", "lat"), lat_first)
    north_b = lax.ppermute(rows_b, ("lon", "lat"), lat_second)

    turn_centre, turn_face = turning(lax.axis_index("lat"))
    levels_scratch = pltpu.VMEM((LEVELS, 2, TALL, LANES), f32)
    return pl.pallas_call(
        ocean_steps,
        out_shape=(
            jax.ShapeDtypeStruct(level_block, f32),
            jax.ShapeDtypeStruct(level_block, f32),
            jax.ShapeDtypeStruct((ROWS, LANES), f32),
        ),
        scratch_shapes=[levels_scratch] * 5
        + [
            pltpu.VMEM((16, 2, TALL, LANES), f32),
            pltpu.VMEM((2, 2, TALL, LANES), f32),
            pltpu.VMEM((2, 2, TALL, LANES), f32),
            pltpu.VMEM((2, TALL, LANES), f32),
        ],
        compiler_params=params,
    )(own, east_a, east_b, north_a, north_b, turn_centre, turn_face)


def solution(mesh):
    return jax.shard_map(
        shards,
        mesh=mesh,
        in_specs=(
            P(None, "lat", "lon"),
            P(None, "lat", "lon"),
            P(None, "lat", "lon"),
            P("lat", "lon"),
            P(None, "lat", "lon"),
            P("lat", "lon"),
        ),
        out_specs=(P(None, "lat", "lon"), P(None, "lat", "lon"), P("lat", "lon")),
        check_vma=False,
    )
```

```python
import math

import jax
import jax.numpy as jnp
from jax import lax
from jax.experimental import pallas as pl
from jax.experimental.pallas import tpu as pltpu
from jax.sharding import PartitionSpec as P

SUBSTEPS = 8
STEPS = 2
LEVELS = 12
ROWS = 96
LANES = 128
HALO = 16
FOLD = 18

PLANES = 3 * LEVELS + 3
BOTTOM, FIRST, SURFACE = 36, 37, 38
PACKS = -(-PLANES // 8)
SENT = PLANES + 2 * PACKS

PAD = 8
EXT = 136
TALL = PAD + EXT + PAD
OWN = HALO
GHOST_A, PATCH, GHOST_B = OWN + ROWS, OWN + ROWS + 1, OWN + ROWS + 1 + FOLD
CHUNKS = ((0, 32), (32, 32), (64, 32), (96, 40))

viscosity = 0.05
friction = 0.1
coriolis = 0.25
substep_time = 0.4
layer = 1.0 / LEVELS
step_time = SUBSTEPS * substep_time
drag = 1.0 / (1.0 + step_time * friction)

VMEM_LIMIT = 24 * 1024 * 1024


def lanes_of(shape):
    return lax.broadcasted_iota(jnp.int32, shape, len(shape) - 1)


def masked_planes(u_ref, v_ref, d_ref, s_ref, m_ref, b_ref, ready):
    lane = lanes_of((ROWS, LANES))
    row = lax.broadcasted_iota(jnp.int32, (ROWS, LANES), 0)
    ready(5)
    ready(4)
    bottom = b_ref[...].astype(jnp.float32)
    first = bottom - jnp.sum(m_ref[...], axis=0).astype(jnp.float32)
    east = jnp.where(lane == LANES - 1, 12.0, pltpu.roll(bottom, LANES - 1, 1))
    north = jnp.where(row == ROWS - 1, 12.0, pltpu.roll(bottom, ROWS - 1, 0))
    up_u, up_v = jnp.minimum(bottom, east), jnp.minimum(bottom, north)
    ready(0)
    for k in range(LEVELS):
        yield k, jnp.where((first <= k) & (up_u > k), u_ref[k], 0.0)
    ready(1)
    for k in range(LEVELS):
        yield LEVELS + k, jnp.where((first <= k) & (up_v > k), v_ref[k], 0.0)
    ready(2)
    running = jnp.zeros_like(bottom)
    for k in range(LEVELS):
        weighted = jnp.where((first <= k) & (bottom > k), d_ref[k], 0.0)
        running = running + weighted
        yield 2 * LEVELS + k, layer * (running - 0.5 * weighted)
    ready(3)
    yield BOTTOM, bottom
    yield FIRST, first
    yield SURFACE, jnp.where(bottom > 0.0, s_ref[...], 0.0)


def strips(u_far, v_far, d_far, s_far, m_far, b_far, a_ref, c_ref, u_ref, v_ref, d_ref, s_ref, m_ref, b_ref, sems):
    pairs = ((u_far, u_ref), (v_far, v_ref), (d_far, d_ref), (s_far, s_ref), (m_far, m_ref), (b_far, b_ref))
    copies = [pltpu.make_async_copy(far, near, sems.at[i]) for i, (far, near) in enumerate(pairs)]
    for i in (5, 4, 0, 1, 2, 3):
        copies[i].start()
    lane = lanes_of((ROWS, LANES))
    even = lax.rem(lax.axis_index("lon"), 2) == 0
    for p, plane in masked_planes(u_ref, v_ref, d_ref, s_ref, m_ref, b_ref, lambda i: copies[i].wait()):
        slot = p % 8
        here = (lane >= HALO * slot) & (lane < HALO * slot + HALO)
        if slot == 0:
            to_east = to_west = jnp.zeros((ROWS, LANES), jnp.float32)
        to_east = jnp.where(here, pltpu.roll(plane, (HALO * slot + HALO) % LANES, 1), to_east)
        to_west = jnp.where(here, pltpu.roll(plane, HALO * slot, 1) if slot else plane, to_west)
        if slot == 7 or p == PLANES - 1:
            a_ref[p // 8] = jnp.where(even, to_east, to_west)
            c_ref[p // 8] = jnp.where(even, to_west, to_east)


def own_block(u_ref, v_ref, d_ref, s_ref, m_ref, b_ref, own_ref):
    for p, plane in masked_planes(u_ref, v_ref, d_ref, s_ref, m_ref, b_ref, lambda i: None):
        own_ref[p] = plane


def outer_rows(low_own, low_a, low_b, top_own, top_a, top_b, a_ref, c_ref):
    even = lax.rem(lax.axis_index("lat"), 2) == 0
    for p in range(SENT):
        if p < PLANES:
            low, top = low_own[p], top_own[p]
        elif p < PLANES + PACKS:
            low, top = low_a[p - PLANES], top_a[p - PLANES]
        else:
            low, top = low_b[p - PLANES - PACKS], top_b[p - PLANES - PACKS]
        a_ref[pl.ds(p * HALO, HALO), :] = jnp.where(even, top[24 - HALO :], low[:HALO])
        c_ref[pl.ds(p * FOLD, FOLD), :] = jnp.where(even, low[:FOLD], top[24 - FOLD :])


def eastward(t0, t1):
    lane = lanes_of(t0.shape)
    r0, r1 = pltpu.roll(t0, LANES - 1, t0.ndim - 1), pltpu.roll(t1, LANES - 1, t0.ndim - 1)
    edge = lane == LANES - 1
    return jnp.where(edge, r1, r0), jnp.where(edge, r0, r1)


def westward(t0, t1):
    lane = lanes_of(t0.shape)
    r0, r1 = pltpu.roll(t0, 1, t0.ndim - 1), pltpu.roll(t1, 1, t0.ndim - 1)
    edge = lane == 0
    return jnp.where(edge, r1, r0), jnp.where(edge, r0, r1)


def fold_ghosts(ref, top, sign=1.0):
    for t in range(2):
        for ghost, source in ((GHOST_A, PATCH + FOLD - 2), (GHOST_B, OWN + ROWS - 2)):
            kept = ref[t, pl.ds(PAD + ghost, 1), :]
            taken = ref[t, pl.ds(PAD + source, 1), :]
            ref[t, pl.ds(PAD + ghost, 1), :] = jnp.where(top, sign * taken, kept)


(BED, FROM, UP_U, LO_U, UP_V, C_U, F_U, G_U, C_V, F_V, G_V, SUM_U, SUM_V, NEW_U, NEW_V, SEA) = range(16)
INNER = (3, 12)
SUMS = (G_U, G_V, NEW_U, NEW_V)


def beyond(p):
    return 12.0 if p in (BOTTOM, FIRST) else 0.0


def beside(east, west, p):
    lane = lanes_of(east.shape)
    slot = HALO * (p % 8)
    e = pltpu.roll(east, LANES - slot, 1) if slot else east
    w = pltpu.roll(west, (2 * LANES - HALO - slot) % LANES, 1) if slot != LANES - HALO else west
    return jnp.where(lane < HALO, e, jnp.where(lane >= LANES - HALO, w, beyond(p)))


def planes_of(pack):
    return range(8 * pack, min(8 * pack + 8, PLANES))


def faces(at, n, flat, ft_ref, fv_ref, top):
    rows, up = pl.ds(PAD + at, n), pl.ds(PAD + at + 1, n)
    bed = [flat[BED, t, rows, :] for t in range(2)]
    start = [flat[FROM, t, rows, :] for t in range(2)]
    bed_east = eastward(*bed)
    start_east = eastward(*start)
    ext_row = lax.broadcasted_iota(jnp.int32, (n, LANES), 0) + at
    mirror = (ext_row >= jnp.where(top, PATCH, EXT)) & (ext_row < PATCH + FOLD)
    for t in range(2):
        up_u = jnp.minimum(bed[t], bed_east[t])
        lo_u = jnp.where(mirror, start_east[t], start[t])
        up_v = jnp.minimum(bed[t], flat[BED, t, up, :])
        count_u = jnp.maximum(up_u - lo_u, 0.0)
        count_v = jnp.maximum(up_v - start[t], 0.0)
        flat[UP_U, t, rows, :] = up_u
        flat[LO_U, t, rows, :] = lo_u
        flat[UP_V, t, rows, :] = up_v
        flat[C_U, t, rows, :] = count_u * (-substep_time * layer)
        flat[C_V, t, rows, :] = count_v * (-substep_time * layer)
        flat[F_U, t, rows, :] = jnp.where(count_u > 0.0, substep_time * ft_ref[rows, :], 0.0)
        flat[F_V, t, rows, :] = jnp.where(count_v > 0.0, -substep_time * fv_ref[rows, :], 0.0)
        flat[SEA, t, rows, :] = jnp.where(bed[t] > 0.0, substep_time, 0.0)


def mask_rows(r, flat, u_all, v_all, flow_u, flow_v):
    rows = pl.ds(pl.multiple_of(r * 8, 8) + PAD, 8)
    for t in range(2):
        lo_u, up_u = flat[LO_U, t, rows, :], flat[UP_U, t, rows, :]
        lo_v, up_v = flat[FROM, t, rows, :], flat[UP_V, t, rows, :]
        us = [jnp.where((lo_u <= k) & (up_u > k), u_all[k, t, rows, :], 0.0) for k in range(LEVELS)]
        vs = [jnp.where((lo_v <= k) & (up_v > k), v_all[k, t, rows, :], 0.0) for k in range(LEVELS)]
        for k in range(LEVELS):
            u_all[k, t, rows, :] = us[k]
            v_all[k, t, rows, :] = vs[k]
        flow_u[0, t, rows, :] = layer * sum(us[1:], us[0])
        flow_v[0, t, rows, :] = layer * sum(vs[1:], vs[0])


def tendencies(r, flat, ft_ref, fv_ref, u_all, v_all, p_all, u_new, v_new):
    base = pl.multiple_of(r * 8, 8) + PAD
    rows, up, down = pl.ds(base, 8), pl.ds(base + 1, 8), pl.ds(base - 1, 8)
    ft, fv = ft_ref[rows, :], fv_ref[rows, :]
    lo_u = [flat[LO_U, t, rows, :] for t in range(2)]
    up_u = [flat[UP_U, t, rows, :] for t in range(2)]
    lo_v = [flat[FROM, t, rows, :] for t in range(2)]
    up_v = [flat[UP_V, t, rows, :] for t in range(2)]
    zero = jnp.zeros((8, LANES), jnp.float32)
    force_u, force_v, total_u, total_v = [zero] * 2, [zero] * 2, [zero] * 2, [zero] * 2
    for k in range(LEVELS):
        eu, wu, ru, ev, wv, rv, u0s, v0s = [], [], [], [], [], [], [], []
        for t in range(2):
            u0, un, us = u_all[k, t, rows, :], u_all[k, t, up, :], u_all[k, t, down, :]
            v0, vn, vs = v_all[k, t, rows, :], v_all[k, t, up, :], v_all[k, t, down, :]
            p0, pn = p_all[k, t, rows, :], p_all[k, t, up, :]
            turn_v = ft * (v0 + vs)
            turn_u = fv * (u0 + un)
            a = viscosity * u0
            c = viscosity * v0
            eu.append(a - p0 + turn_v)
            wu.append(a)
            ru.append(viscosity * (un + us) - 4.0 * a + p0 + turn_v)
            ev.append(c)
            wv.append(c - turn_u)
            rv.append(viscosity * (vn + vs) - 4.0 * c + (p0 - pn) - turn_u)
            u0s.append(u0)
            v0s.append(v0)
        eu, wu, ev, wv = eastward(*eu), westward(*wu), eastward(*ev), westward(*wv)
        for t in range(2):
            tend_u = jnp.where((lo_u[t] <= k) & (up_u[t] > k), eu[t] + wu[t] + ru[t], 0.0)
            tend_v = jnp.where((lo_v[t] <= k) & (up_v[t] > k), ev[t] + wv[t] + rv[t], 0.0)
            force_u[t] = force_u[t] + tend_u
            force_v[t] = force_v[t] + tend_v
            new_u = u0s[t] + step_time * tend_u
            new_v = v0s[t] + step_time * tend_v
            new_u = jnp.where(up_u[t] == k + 1, drag * new_u, new_u)
            new_v = jnp.where(up_v[t] == k + 1, drag * new_v, new_v)
            total_u[t] = total_u[t] + new_u
            total_v[t] = total_v[t] + new_v
            u_new[k, t, rows, :] = new_u
            v_new[k, t, rows, :] = new_v
    for t in range(2):
        flat[G_U, t, rows, :] = (substep_time * layer) * force_u[t]
        flat[G_V, t, rows, :] = (substep_time * layer) * force_v[t]
        flat[NEW_U, t, rows, :] = layer * total_u[t]
        flat[NEW_V, t, rows, :] = layer * total_v[t]


def inner_rows(own_ref, ea_ref, eb_ref, ft_ref, fv_ref, u_all, v_all, p_all, u_new, v_new, sums, bed, start, flow_u, flow_v, height, flat):
    even_lon = lax.rem(lax.axis_index("lon"), 2) == 0
    place = [u_all.at[k] for k in range(LEVELS)] + [v_all.at[k] for k in range(LEVELS)]
    place += [p_all.at[k] for k in range(LEVELS)] + [flat.at[BED], flat.at[FROM], height]
    for pack in range(PACKS):
        for at in range(0, ROWS, 32):
            a, b = ea_ref[pack, pl.ds(at, 32), :], eb_ref[pack, pl.ds(at, 32), :]
            east, west = jnp.where(even_lon, a, b), jnp.where(even_lon, b, a)
            tiles = [beside(east, west, p) for p in planes_of(pack)]
            for p, tile in zip(planes_of(pack), tiles):
                place[p][0, pl.ds(PAD + OWN + at, 32), :] = own_ref[p, pl.ds(at, 32), :]
                place[p][1, pl.ds(PAD + OWN + at, 32), :] = tile
    faces(OWN, 48, flat, ft_ref, fv_ref, False)
    faces(OWN + 48, 40, flat, ft_ref, fv_ref, False)

    def first(r, carry):
        mask_rows(r, flat, u_all, v_all, flow_u, flow_v)
        return carry

    def second(r, carry):
        tendencies(r, flat, ft_ref, fv_ref, u_all, v_all, p_all, u_new, v_new)
        return carry

    lax.fori_loop(INNER[0] - 1, INNER[1] + 1, first, 0)
    lax.fori_loop(INNER[0], INNER[1], second, 0)
    own = pl.ds(PAD + OWN, ROWS)
    inner = pl.ds(PAD + 8 * INNER[0], 8 * (INNER[1] - INNER[0]))
    for t in range(2):
        bed[t, own, :] = flat[BED, t, own, :]
        start[t, own, :] = flat[FROM, t, own, :]
        for i, which in enumerate(SUMS):
            sums[i, t, inner, :] = flat[which, t, inner, :]


def ocean_steps(
    na_ref, nb_ref, ft_ref, fv_ref, u_in, v_in, p_in, u_done, v_done, sums, bed, start, flow_u_in, flow_v_in, height_in,
    u_out, v_out, h_out,
    u_all, v_all, p_all, u_new, v_new,
    flat, flow_u, flow_v, height,
):
    lat = lax.axis_index("lat")
    even_lat = lax.rem(lat, 2) == 0
    even_lon = lax.rem(lax.axis_index("lon"), 2) == 0
    top = lat == lax.axis_size("lat") - 1
    place = [u_all.at[k] for k in range(LEVELS)] + [v_all.at[k] for k in range(LEVELS)]
    place += [p_all.at[k] for k in range(LEVELS)] + [flat.at[BED], flat.at[FROM], height]

    def north_rows(p):
        return jnp.where(even_lat, na_ref[pl.ds(p * HALO, HALO), :], nb_ref[pl.ds(p * FOLD, HALO), :])

    def south_rows(p):
        return jnp.where(even_lat, nb_ref[pl.ds(p * FOLD + FOLD - HALO, HALO), :], na_ref[pl.ds(p * HALO, HALO), :])

    own = pl.ds(PAD + OWN, ROWS)
    low = pl.ds(PAD + OWN, 8 * (INNER[0] + 1) - OWN)
    high = pl.ds(PAD + 8 * (INNER[1] - 1), OWN + ROWS - 8 * (INNER[1] - 1))
    inner = pl.ds(PAD + 8 * INNER[0], 8 * (INNER[1] - INNER[0]))
    masked = pl.ds(PAD + 8 * (INNER[0] - 1), 8 * (INNER[1] - INNER[0] + 2))
    for t in range(2):
        for k in range(LEVELS):
            p_all[k, t, own, :] = p_in[k, t, own, :]
            for rows in (low, high):
                u_all[k, t, rows, :] = u_in[k, t, rows, :]
                v_all[k, t, rows, :] = v_in[k, t, rows, :]
        flat[BED, t, own, :] = bed[t, own, :]
        flat[FROM, t, own, :] = start[t, own, :]
        height[t, own, :] = height_in[t, own, :]
        flow_u[0, t, masked, :] = flow_u_in[0, t, masked, :]
        flow_v[0, t, masked, :] = flow_v_in[0, t, masked, :]
        for i, which in enumerate(SUMS):
            flat[which, t, inner, :] = sums[i, t, inner, :]
            flat[which, t, pl.ds(PAD + EXT - 8, 8), :] = jnp.zeros((8, LANES), jnp.float32)

    edge, after = pl.ds(0, PAD), pl.ds(PAD + OWN + ROWS + HALO, 16)
    for pack in range(PACKS):
        pa, pb = PLANES + pack, PLANES + PACKS + pack
        for rows, at in ((south_rows, PAD), (north_rows, PAD + OWN + ROWS)):
            a, b = rows(pa), rows(pb)
            east, west = jnp.where(even_lon, a, b), jnp.where(even_lon, b, a)
            tiles = [(rows(p), beside(east, west, p)) for p in planes_of(pack)]
            for p, (t0, t1) in zip(planes_of(pack), tiles):
                place[p][0, pl.ds(at, HALO), :] = t0
                place[p][1, pl.ds(at, HALO), :] = t1
        for p in planes_of(pack):
            for t in range(2):
                place[p][t, edge, :] = jnp.full((PAD, LANES), beyond(p), jnp.float32)
                place[p][t, after, :] = jnp.full((16, LANES), beyond(p), jnp.float32)

    @pl.when(top)
    def _():
        lane = lanes_of((24, LANES))

        def flipped(x):
            return jnp.take_along_axis(x, LANES - 1 - lane, axis=1)

        for pack in range(PACKS):
            a = flipped(nb_ref[pl.ds((PLANES + pack) * FOLD, 24), :])
            b = flipped(nb_ref[pl.ds((PLANES + PACKS + pack) * FOLD, 24), :])
            east, west = jnp.where(even_lon, b, a), jnp.where(even_lon, a, b)
            tiles = []
            for p in planes_of(pack):
                slot = HALO * (p % 8)
                e = pltpu.roll(west, (slot + HALO) % LANES, 1) if slot != LANES - HALO else west
                w = pltpu.roll(east, slot, 1) if slot else east
                t0 = flipped(nb_ref[pl.ds(p * FOLD, 24), :])
                t1 = jnp.where(lane < HALO, e, jnp.where(lane >= LANES - HALO, w, beyond(p)))
                if p < LEVELS:
                    t0, t1 = eastward(t0, t1)
                    t0, t1 = -t0, -t1
                tiles.append((t0, t1))
            for p, (t0, t1) in zip(planes_of(pack), tiles):
                place[p][0, pl.ds(PAD + PATCH, FOLD), :] = t0[:FOLD]
                place[p][1, pl.ds(PAD + PATCH, FOLD), :] = t1[:FOLD]

    fold_ghosts(flat.at[BED], top)
    for at, n in CHUNKS:
        faces(at, n, flat, ft_ref, fv_ref, top)
    for flow in (flow_u, flow_v):
        for now in range(2):
            for t in range(2):
                flow[now, t, edge, :] = jnp.zeros((PAD, LANES), jnp.float32)
                flow[now, t, pl.ds(PAD + EXT, PAD), :] = jnp.zeros((PAD, LANES), jnp.float32)

    def mask_first(r, carry):
        mask_rows(r, flat, u_all, v_all, flow_u, flow_v)
        return carry

    lax.fori_loop(0, INNER[0] - 1, mask_first, 0)
    lax.fori_loop(INNER[1] + 1, EXT // 8, mask_first, 0)

    for step in range(STEPS):
        last = step == STEPS - 1
        for k in range(LEVELS):
            fold_ghosts(u_all.at[k], top)
            fold_ghosts(v_all.at[k], top, -1.0)
            if step == 0:
                fold_ghosts(p_all.at[k], top)
        fold_ghosts(flow_u.at[0], top)

        def tend(r, carry):
            tendencies(r, flat, ft_ref, fv_ref, u_all, v_all, p_all, u_new, v_new)
            return carry

        if last:
            lax.fori_loop(1, jnp.where(top, EXT // 8, EXT // 8 - 2), tend, 0)
        else:
            lax.fori_loop(0, INNER[0], tend, 0)
            lax.fori_loop(INNER[1], jnp.where(top, EXT // 8, EXT // 8 - 1), tend, 0)
        for which in (SUM_U, SUM_V):
            for t in range(2):
                flat[which, t, pl.ds(PAD, EXT), :] = jnp.zeros((EXT, LANES), jnp.float32)

        def substep(now, later):
            for at, n in CHUNKS:
                rows, down = pl.ds(PAD + at, n), pl.ds(PAD + at - 1, n)
                u = [flow_u[now, t, rows, :] for t in range(2)]
                uw = westward(*u)
                for t in range(2):
                    spread = u[t] - uw[t] + flow_v[now, t, rows, :] - flow_v[now, t, down, :]
                    height[t, rows, :] = height[t, rows, :] - flat[SEA, t, rows, :] * spread
            fold_ghosts(height, top)
            for at, n in CHUNKS:
                rows, up, down = pl.ds(PAD + at, n), pl.ds(PAD + at + 1, n), pl.ds(PAD + at - 1, n)
                h = [height[t, rows, :] for t in range(2)]
                he = eastward(*h)
                qv = [flow_v[now, t, rows, :] + flow_v[now, t, down, :] for t in range(2)]
                qve = eastward(*qv)
                qu = [flow_u[now, t, rows, :] + flow_u[now, t, up, :] for t in range(2)]
                quw = westward(*qu)
                for t in range(2):
                    next_u = (
                        flow_u[now, t, rows, :]
                        + flat[C_U, t, rows, :] * (he[t] - h[t])
                        + flat[F_U, t, rows, :] * (qv[t] + qve[t])
                        + flat[G_U, t, rows, :]
                    )
                    next_v = (
                        flow_v[now, t, rows, :]
                        + flat[C_V, t, rows, :] * (height[t, up, :] - h[t])
                        + flat[F_V, t, rows, :] * (qu[t] + quw[t])
                        + flat[G_V, t, rows, :]
                    )
                    flow_u[later, t, rows, :] = next_u
                    flow_v[later, t, rows, :] = next_v
                    flat[SUM_U, t, rows, :] = flat[SUM_U, t, rows, :] + next_u
                    flat[SUM_V, t, rows, :] = flat[SUM_V, t, rows, :] + next_v
            fold_ghosts(flow_u.at[later], top)

        def two_substeps(turn, carry):
            substep(0, 1)
            substep(1, 0)
            return carry

        lax.fori_loop(0, SUBSTEPS // 2, two_substeps, 0)

        def correct(r, u_from, v_from):
            rows = pl.ds(pl.multiple_of(r * 8, 8) + PAD, 8)
            for t in range(1 if last else 2):
                lo_u, up_u = flat[LO_U, t, rows, :], flat[UP_U, t, rows, :]
                lo_v, up_v = flat[FROM, t, rows, :], flat[UP_V, t, rows, :]
                mean_u = flat[SUM_U, t, rows, :] / SUBSTEPS
                mean_v = flat[SUM_V, t, rows, :] / SUBSTEPS
                depth_u = layer * jnp.maximum(up_u - lo_u, 1.0)
                depth_v = layer * jnp.maximum(up_v - lo_v, 1.0)
                add_u = (mean_u - flat[NEW_U, t, rows, :]) / depth_u
                add_v = (mean_v - flat[NEW_V, t, rows, :]) / depth_v
                us = [jnp.where((lo_u <= k) & (up_u > k), u_from[k, t, rows, :] + add_u, 0.0) for k in range(LEVELS)]
                vs = [jnp.where((lo_v <= k) & (up_v > k), v_from[k, t, rows, :] + add_v, 0.0) for k in range(LEVELS)]
                for k in range(LEVELS):
                    if last:
                        out = pl.ds(pl.multiple_of(r * 8 - OWN, 8), 8)
                        u_out[k, out, :] = us[k]
                        v_out[k, out, :] = vs[k]
                    else:
                        u_all[k, t, rows, :] = us[k]
                        v_all[k, t, rows, :] = vs[k]
                if not last:
                    flow_u[0, t, rows, :] = mean_u
                    flow_v[0, t, rows, :] = mean_v

        def correct_here(r, carry):
            correct(r, u_new, v_new)
            return carry

        def correct_inner(r, carry):
            correct(r, u_done, v_done)
            return carry

        if last:
            lax.fori_loop(OWN // 8, (OWN + ROWS) // 8, correct_here, 0)
        else:
            lax.fori_loop(0, INNER[0], correct_here, 0)
            lax.fori_loop(INNER[0], INNER[1], correct_inner, 0)
            lax.fori_loop(INNER[1], EXT // 8, correct_here, 0)

    h_out[...] = height[0, pl.ds(PAD + OWN, ROWS), :]


def lon_swaps():
    count = lax.axis_size("lon")
    first = [(i, i ^ 1) for i in range(count)]
    second = [(i, (((i + 1) % count) ^ 1) - 1) for i in range(count)]
    return first, [(i, j % count) for i, j in second]


def lat_swaps():
    lats, lons = lax.axis_size("lat"), lax.axis_size("lon")
    first, second = [], []
    for lat in range(lats):
        for lon in range(lons):
            first.append((lon * lats + lat, lon * lats + (lat ^ 1)))
            if lat == lats - 1:
                second.append((lon * lats + lat, (lons - 1 - lon) * lats + lat))
            elif lat:
                second.append((lon * lats + lat, lon * lats + ((lat + 1) ^ 1) - 1))
    return first, second


def turning(lat):
    lats = lax.axis_size("lat")
    ext = jnp.arange(TALL, dtype=jnp.int32) - PAD
    mirror = (lat == lats - 1) & (ext >= PATCH)
    row = jnp.where(mirror, lats * ROWS - FOLD + ext - PATCH, lat * ROWS + ext - OWN).astype(jnp.float32)
    sign = jnp.where(mirror, -0.25 * coriolis, 0.25 * coriolis)
    cells = lats * ROWS
    centre = sign * jnp.sin(math.pi * ((row + 0.5) / cells - 0.5))
    face = sign * jnp.sin(math.pi * ((row + 1.0) / cells - 0.5))
    wide = (TALL, LANES)
    return jnp.broadcast_to(centre[:, None], wide), jnp.broadcast_to(face[:, None], wide)


def whole(*shape):
    return pl.BlockSpec(shape, lambda *_: (0,) * len(shape))


def shards(u_velocity, v_velocity, density, surface, land_mask, bottom):
    f32 = jnp.float32
    params = pltpu.CompilerParams(vmem_limit_bytes=VMEM_LIMIT)
    level_block = (LEVELS, ROWS, LANES)
    fields = (u_velocity, v_velocity, density, surface, land_mask, bottom)
    pack_a, pack_b = pl.pallas_call(
        strips,
        out_shape=(jax.ShapeDtypeStruct((PACKS, ROWS, LANES), f32),) * 2,
        in_specs=[pl.BlockSpec(memory_space=pltpu.HBM)] * 6,
        scratch_shapes=[pltpu.VMEM(level_block, f32)] * 3
        + [pltpu.VMEM((ROWS, LANES), f32), pltpu.VMEM(level_block, jnp.int32), pltpu.VMEM((ROWS, LANES), jnp.int32)]
        + [pltpu.SemaphoreType.DMA((6,))],
        compiler_params=pltpu.CompilerParams(vmem_limit_bytes=56 * 1024 * 1024),
    )(*fields)
    lon_first, lon_second = lon_swaps()
    east_a = lax.ppermute(pack_a, "lon", lon_first)
    east_b = lax.ppermute(pack_b, "lon", lon_second)
    own = pl.pallas_call(
        own_block,
        out_shape=jax.ShapeDtypeStruct((PLANES, ROWS, LANES), f32),
        compiler_params=pltpu.CompilerParams(vmem_limit_bytes=8 * 1024 * 1024),
        cost_estimate=pl.CostEstimate(flops=4000000, bytes_accessed=5000000, transcendentals=0),
    )(*fields)

    low = lambda planes: pl.BlockSpec((planes, 24, LANES), lambda i: (0, 0, 0))
    high = lambda planes: pl.BlockSpec((planes, 24, LANES), lambda i: (0, ROWS // 24 - 1, 0))
    rows_a, rows_b = pl.pallas_call(
        outer_rows,
        grid=(1,),
        in_specs=[low(PLANES), low(PACKS), low(PACKS), high(PLANES), high(PACKS), high(PACKS)],
        out_specs=(whole(SENT * HALO, LANES), whole(888, LANES)),
        out_shape=(
            jax.ShapeDtypeStruct((SENT * HALO, LANES), f32),
            jax.ShapeDtypeStruct((888, LANES), f32),
        ),
        compiler_params=params,
    )(own, east_a, east_b, own, east_a, east_b)
    lat_first, lat_second = lat_swaps()
    north_b = lax.ppermute(rows_b, ("lon", "lat"), lat_second)
    north_a = lax.ppermute(rows_a, ("lon", "lat"), lat_first)

    turn_centre, turn_face = turning(lax.axis_index("lat"))
    levels, pair, single = (LEVELS, 2, TALL, LANES), (2, 2, TALL, LANES), (2, TALL, LANES)
    shapes = [levels] * 5 + [(len(SUMS), 2, TALL, LANES), single, single, (1, 2, TALL, LANES), (1, 2, TALL, LANES), single]
    done = pl.pallas_call(
        inner_rows,
        out_shape=tuple(jax.ShapeDtypeStruct(shape, f32) for shape in shapes),
        scratch_shapes=[pltpu.VMEM((16, 2, TALL, LANES), f32)],
        compiler_params=params,
        cost_estimate=pl.CostEstimate(flops=40000000, bytes_accessed=12000000, transcendentals=0),
    )(own, east_a, east_b, turn_centre, turn_face)
    return pl.pallas_call(
        ocean_steps,
        out_shape=(
            jax.ShapeDtypeStruct(level_block, f32),
            jax.ShapeDtypeStruct(level_block, f32),
            jax.ShapeDtypeStruct((ROWS, LANES), f32),
        ),
        scratch_shapes=[pltpu.VMEM(levels, f32)] * 5
        + [pltpu.VMEM((16, 2, TALL, LANES), f32)]
        + [pltpu.VMEM(pair, f32), pltpu.VMEM(pair, f32), pltpu.VMEM(single, f32)],
        compiler_params=params,
    )(north_a, north_b, turn_centre, turn_face, *done)


def solution(mesh):
    return jax.shard_map(
        shards,
        mesh=mesh,
        in_specs=(
            P(None, "lat", "lon"),
            P(None, "lat", "lon"),
            P(None, "lat", "lon"),
            P("lat", "lon"),
            P(None, "lat", "lon"),
            P("lat", "lon"),
        ),
        out_specs=(P(None, "lat", "lon"), P(None, "lat", "lon"), P("lat", "lon")),
        check_vma=False,
    )
```

```python
import math

import jax
import jax.numpy as jnp
from jax import lax
from jax.experimental import pallas as pl
from jax.experimental.pallas import tpu as pltpu
from jax.sharding import PartitionSpec as P

SUBSTEPS = 8
STEPS = 2
LEVELS = 12
ROWS = 96
LANES = 128
HALO = 16
FOLD = 18

PLANES = 3 * LEVELS + 3
BOTTOM, FIRST, SURFACE = 36, 37, 38
PACKS = -(-PLANES // 8)
SENT = PLANES + 2 * PACKS

PAD = 8
EXT = 136
TALL = PAD + EXT + PAD
OWN = HALO
GHOST_A, PATCH, GHOST_B = OWN + ROWS, OWN + ROWS + 1, OWN + ROWS + 1 + FOLD
CHUNKS = ((0, 32), (32, 32), (64, 32), (96, 40))

viscosity = 0.05
friction = 0.1
coriolis = 0.25
substep_time = 0.4
layer = 1.0 / LEVELS
step_time = SUBSTEPS * substep_time
drag = 1.0 / (1.0 + step_time * friction)

VMEM_LIMIT = 24 * 1024 * 1024


def lanes_of(shape):
    return lax.broadcasted_iota(jnp.int32, shape, len(shape) - 1)


def masked_planes(u_ref, v_ref, d_ref, s_ref, m_ref, b_ref, ready):
    lane = lanes_of((ROWS, LANES))
    row = lax.broadcasted_iota(jnp.int32, (ROWS, LANES), 0)
    ready(5)
    ready(4)
    bottom = b_ref[...].astype(jnp.float32)
    first = bottom - jnp.sum(m_ref[...], axis=0).astype(jnp.float32)
    east = jnp.where(lane == LANES - 1, 12.0, pltpu.roll(bottom, LANES - 1, 1))
    north = jnp.where(row == ROWS - 1, 12.0, pltpu.roll(bottom, ROWS - 1, 0))
    up_u, up_v = jnp.minimum(bottom, east), jnp.minimum(bottom, north)
    ready(0)
    for k in range(LEVELS):
        yield k, jnp.where((first <= k) & (up_u > k), u_ref[k], 0.0)
    ready(1)
    for k in range(LEVELS):
        yield LEVELS + k, jnp.where((first <= k) & (up_v > k), v_ref[k], 0.0)
    ready(2)
    running = jnp.zeros_like(bottom)
    for k in range(LEVELS):
        weighted = jnp.where((first <= k) & (bottom > k), d_ref[k], 0.0)
        running = running + weighted
        yield 2 * LEVELS + k, layer * (running - 0.5 * weighted)
    ready(3)
    yield BOTTOM, bottom
    yield FIRST, first
    yield SURFACE, jnp.where(bottom > 0.0, s_ref[...], 0.0)


def strips(u_far, v_far, d_far, s_far, m_far, b_far, a_ref, c_ref, u_ref, v_ref, d_ref, s_ref, m_ref, b_ref, sems):
    pairs = ((u_far, u_ref), (v_far, v_ref), (d_far, d_ref), (s_far, s_ref), (m_far, m_ref), (b_far, b_ref))
    copies = [pltpu.make_async_copy(far, near, sems.at[i]) for i, (far, near) in enumerate(pairs)]
    for i in (5, 4, 0, 1, 2, 3):
        copies[i].start()
    lane = lanes_of((ROWS, LANES))
    even = lax.rem(lax.axis_index("lon"), 2) == 0
    for p, plane in masked_planes(u_ref, v_ref, d_ref, s_ref, m_ref, b_ref, lambda i: copies[i].wait()):
        slot = p % 8
        here = (lane >= HALO * slot) & (lane < HALO * slot + HALO)
        if slot == 0:
            to_east = to_west = jnp.zeros((ROWS, LANES), jnp.float32)
        to_east = jnp.where(here, pltpu.roll(plane, (HALO * slot + HALO) % LANES, 1), to_east)
        to_west = jnp.where(here, pltpu.roll(plane, HALO * slot, 1) if slot else plane, to_west)
        if slot == 7 or p == PLANES - 1:
            a_ref[p // 8] = jnp.where(even, to_east, to_west)
            c_ref[p // 8] = jnp.where(even, to_west, to_east)


def own_block(u_ref, v_ref, d_ref, s_ref, m_ref, b_ref, own_ref):
    for p, plane in masked_planes(u_ref, v_ref, d_ref, s_ref, m_ref, b_ref, lambda i: None):
        own_ref[p] = plane


def outer_rows(low_own, low_a, low_b, top_own, top_a, top_b, a_ref, c_ref):
    even = lax.rem(lax.axis_index("lat"), 2) == 0
    for p in range(SENT):
        if p < PLANES:
            low, top = low_own[p], top_own[p]
        elif p < PLANES + PACKS:
            low, top = low_a[p - PLANES], top_a[p - PLANES]
        else:
            low, top = low_b[p - PLANES - PACKS], top_b[p - PLANES - PACKS]
        a_ref[pl.ds(p * HALO, HALO), :] = jnp.where(even, top[24 - HALO :], low[:HALO])
        c_ref[pl.ds(p * FOLD, FOLD), :] = jnp.where(even, low[:FOLD], top[24 - FOLD :])


def eastward(t0, t1):
    lane = lanes_of(t0.shape)
    r0, r1 = pltpu.roll(t0, LANES - 1, t0.ndim - 1), pltpu.roll(t1, LANES - 1, t0.ndim - 1)
    edge = lane == LANES - 1
    return jnp.where(edge, r1, r0), jnp.where(edge, r0, r1)


def westward(t0, t1):
    lane = lanes_of(t0.shape)
    r0, r1 = pltpu.roll(t0, 1, t0.ndim - 1), pltpu.roll(t1, 1, t0.ndim - 1)
    edge = lane == 0
    return jnp.where(edge, r1, r0), jnp.where(edge, r0, r1)


def fold_ghosts(ref, top, sign=1.0):
    for t in range(2):
        for ghost, source in ((GHOST_A, PATCH + FOLD - 2), (GHOST_B, OWN + ROWS - 2)):
            kept = ref[t, pl.ds(PAD + ghost, 1), :]
            taken = ref[t, pl.ds(PAD + source, 1), :]
            ref[t, pl.ds(PAD + ghost, 1), :] = jnp.where(top, sign * taken, kept)


(BED, FROM, UP_U, LO_U, UP_V, C_U, F_U, G_U, C_V, F_V, G_V, SUM_U, SUM_V, NEW_U, NEW_V, SEA) = range(16)
INNER = (3, 12)
CORE = (4, 11)
CORE_ROWS = (8 * CORE[0], 8 * (CORE[1] - CORE[0]))
INNER_CHUNKS = ((24, 32), (56, 40))
OUTER_CHUNKS = ((0, 40), (80, 24), (104, 32))
SUMS = (G_U, G_V, NEW_U, NEW_V)


def beyond(p):
    return 12.0 if p in (BOTTOM, FIRST) else 0.0


def beside(east, west, p):
    lane = lanes_of(east.shape)
    slot = HALO * (p % 8)
    e = pltpu.roll(east, LANES - slot, 1) if slot else east
    w = pltpu.roll(west, (2 * LANES - HALO - slot) % LANES, 1) if slot != LANES - HALO else west
    return jnp.where(lane < HALO, e, jnp.where(lane >= LANES - HALO, w, beyond(p)))


def planes_of(pack):
    return range(8 * pack, min(8 * pack + 8, PLANES))


def faces(at, n, flat, ft_ref, fv_ref, top):
    rows, up = pl.ds(PAD + at, n), pl.ds(PAD + at + 1, n)
    bed = [flat[BED, t, rows, :] for t in range(2)]
    start = [flat[FROM, t, rows, :] for t in range(2)]
    bed_east = eastward(*bed)
    start_east = eastward(*start)
    ext_row = lax.broadcasted_iota(jnp.int32, (n, LANES), 0) + at
    mirror = (ext_row >= jnp.where(top, PATCH, EXT)) & (ext_row < PATCH + FOLD)
    for t in range(2):
        up_u = jnp.minimum(bed[t], bed_east[t])
        lo_u = jnp.where(mirror, start_east[t], start[t])
        up_v = jnp.minimum(bed[t], flat[BED, t, up, :])
        count_u = jnp.maximum(up_u - lo_u, 0.0)
        count_v = jnp.maximum(up_v - start[t], 0.0)
        flat[UP_U, t, rows, :] = up_u
        flat[LO_U, t, rows, :] = lo_u
        flat[UP_V, t, rows, :] = up_v
        flat[C_U, t, rows, :] = count_u * (-substep_time * layer)
        flat[C_V, t, rows, :] = count_v * (-substep_time * layer)
        flat[F_U, t, rows, :] = jnp.where(count_u > 0.0, substep_time * ft_ref[rows, :], 0.0)
        flat[F_V, t, rows, :] = jnp.where(count_v > 0.0, -substep_time * fv_ref[rows, :], 0.0)
        flat[SEA, t, rows, :] = jnp.where(bed[t] > 0.0, substep_time, 0.0)


def mask_rows(r, flat, u_all, v_all, flow_u, flow_v):
    rows = pl.ds(pl.multiple_of(r * 8, 8) + PAD, 8)
    for t in range(2):
        lo_u, up_u = flat[LO_U, t, rows, :], flat[UP_U, t, rows, :]
        lo_v, up_v = flat[FROM, t, rows, :], flat[UP_V, t, rows, :]
        us = [jnp.where((lo_u <= k) & (up_u > k), u_all[k, t, rows, :], 0.0) for k in range(LEVELS)]
        vs = [jnp.where((lo_v <= k) & (up_v > k), v_all[k, t, rows, :], 0.0) for k in range(LEVELS)]
        for k in range(LEVELS):
            u_all[k, t, rows, :] = us[k]
            v_all[k, t, rows, :] = vs[k]
        flow_u[0, t, rows, :] = layer * sum(us[1:], us[0])
        flow_v[0, t, rows, :] = layer * sum(vs[1:], vs[0])


def tendencies(r, flat, ft_ref, fv_ref, u_all, v_all, p_all, u_new, v_new):
    base = pl.multiple_of(r * 8, 8) + PAD
    rows, up, down = pl.ds(base, 8), pl.ds(base + 1, 8), pl.ds(base - 1, 8)
    ft, fv = ft_ref[rows, :], fv_ref[rows, :]
    lo_u = [flat[LO_U, t, rows, :] for t in range(2)]
    up_u = [flat[UP_U, t, rows, :] for t in range(2)]
    lo_v = [flat[FROM, t, rows, :] for t in range(2)]
    up_v = [flat[UP_V, t, rows, :] for t in range(2)]
    zero = jnp.zeros((8, LANES), jnp.float32)
    force_u, force_v, total_u, total_v = [zero] * 2, [zero] * 2, [zero] * 2, [zero] * 2
    for k in range(LEVELS):
        eu, wu, ru, ev, wv, rv, u0s, v0s = [], [], [], [], [], [], [], []
        for t in range(2):
            u0, un, us = u_all[k, t, rows, :], u_all[k, t, up, :], u_all[k, t, down, :]
            v0, vn, vs = v_all[k, t, rows, :], v_all[k, t, up, :], v_all[k, t, down, :]
            p0, pn = p_all[k, t, rows, :], p_all[k, t, up, :]
            turn_v = ft * (v0 + vs)
            turn_u = fv * (u0 + un)
            a = viscosity * u0
            c = viscosity * v0
            eu.append(a - p0 + turn_v)
            wu.append(a)
            ru.append(viscosity * (un + us) - 4.0 * a + p0 + turn_v)
            ev.append(c)
            wv.append(c - turn_u)
            rv.append(viscosity * (vn + vs) - 4.0 * c + (p0 - pn) - turn_u)
            u0s.append(u0)
            v0s.append(v0)
        eu, wu, ev, wv = eastward(*eu), westward(*wu), eastward(*ev), westward(*wv)
        for t in range(2):
            tend_u = jnp.where((lo_u[t] <= k) & (up_u[t] > k), eu[t] + wu[t] + ru[t], 0.0)
            tend_v = jnp.where((lo_v[t] <= k) & (up_v[t] > k), ev[t] + wv[t] + rv[t], 0.0)
            force_u[t] = force_u[t] + tend_u
            force_v[t] = force_v[t] + tend_v
            new_u = u0s[t] + step_time * tend_u
            new_v = v0s[t] + step_time * tend_v
            new_u = jnp.where(up_u[t] == k + 1, drag * new_u, new_u)
            new_v = jnp.where(up_v[t] == k + 1, drag * new_v, new_v)
            total_u[t] = total_u[t] + new_u
            total_v[t] = total_v[t] + new_v
            u_new[k, t, rows, :] = new_u
            v_new[k, t, rows, :] = new_v
    for t in range(2):
        flat[G_U, t, rows, :] = (substep_time * layer) * force_u[t]
        flat[G_V, t, rows, :] = (substep_time * layer) * force_v[t]
        flat[NEW_U, t, rows, :] = layer * total_u[t]
        flat[NEW_V, t, rows, :] = layer * total_v[t]


def substep(now, later, chunks, top, flat, flow_u, flow_v, height):
    for at, n in chunks:
        rows, down = pl.ds(PAD + at, n), pl.ds(PAD + at - 1, n)
        u = [flow_u[now, t, rows, :] for t in range(2)]
        uw = westward(*u)
        for t in range(2):
            spread = u[t] - uw[t] + flow_v[now, t, rows, :] - flow_v[now, t, down, :]
            height[t, rows, :] = height[t, rows, :] - flat[SEA, t, rows, :] * spread
    if top is not None:
        fold_ghosts(height, top)
    for at, n in chunks:
        rows, up, down = pl.ds(PAD + at, n), pl.ds(PAD + at + 1, n), pl.ds(PAD + at - 1, n)
        h = [height[t, rows, :] for t in range(2)]
        he = eastward(*h)
        qv = [flow_v[now, t, rows, :] + flow_v[now, t, down, :] for t in range(2)]
        qve = eastward(*qv)
        qu = [flow_u[now, t, rows, :] + flow_u[now, t, up, :] for t in range(2)]
        quw = westward(*qu)
        for t in range(2):
            next_u = (
                flow_u[now, t, rows, :]
                + flat[C_U, t, rows, :] * (he[t] - h[t])
                + flat[F_U, t, rows, :] * (qv[t] + qve[t])
                + flat[G_U, t, rows, :]
            )
            next_v = (
                flow_v[now, t, rows, :]
                + flat[C_V, t, rows, :] * (height[t, up, :] - h[t])
                + flat[F_V, t, rows, :] * (qu[t] + quw[t])
                + flat[G_V, t, rows, :]
            )
            flow_u[later, t, rows, :] = next_u
            flow_v[later, t, rows, :] = next_v
            flat[SUM_U, t, rows, :] = flat[SUM_U, t, rows, :] + next_u
            flat[SUM_V, t, rows, :] = flat[SUM_V, t, rows, :] + next_v
    if top is not None:
        fold_ghosts(flow_u.at[later], top)


def substeps(chunks, top, flat, flow_u, flow_v, height):
    for which in (SUM_U, SUM_V):
        for t in range(2):
            for at, n in chunks:
                flat[which, t, pl.ds(PAD + at, n), :] = jnp.zeros((n, LANES), jnp.float32)

    def two(turn, carry):
        substep(0, 1, chunks, top, flat, flow_u, flow_v, height)
        substep(1, 0, chunks, top, flat, flow_u, flow_v, height)
        return carry

    lax.fori_loop(0, SUBSTEPS // 2, two, 0)


def correct(first, end, flat, u_from, v_from, u_to, v_to, flow_u, flow_v):
    def tile(r, carry):
        rows = pl.ds(pl.multiple_of(r * 8, 8) + PAD, 8)
        last = flow_u is None
        for t in range(1 if last else 2):
            lo_u, up_u = flat[LO_U, t, rows, :], flat[UP_U, t, rows, :]
            lo_v, up_v = flat[FROM, t, rows, :], flat[UP_V, t, rows, :]
            mean_u = flat[SUM_U, t, rows, :] / SUBSTEPS
            mean_v = flat[SUM_V, t, rows, :] / SUBSTEPS
            depth_u = layer * jnp.maximum(up_u - lo_u, 1.0)
            depth_v = layer * jnp.maximum(up_v - lo_v, 1.0)
            add_u = (mean_u - flat[NEW_U, t, rows, :]) / depth_u
            add_v = (mean_v - flat[NEW_V, t, rows, :]) / depth_v
            us = [jnp.where((lo_u <= k) & (up_u > k), u_from[k, t, rows, :] + add_u, 0.0) for k in range(LEVELS)]
            vs = [jnp.where((lo_v <= k) & (up_v > k), v_from[k, t, rows, :] + add_v, 0.0) for k in range(LEVELS)]
            for k in range(LEVELS):
                if last:
                    out = pl.ds(pl.multiple_of(r * 8 - OWN, 8), 8)
                    u_to[k, out, :] = us[k]
                    v_to[k, out, :] = vs[k]
                else:
                    u_to[k, t, rows, :] = us[k]
                    v_to[k, t, rows, :] = vs[k]
            if not last:
                flow_u[0, t, rows, :] = mean_u
                flow_v[0, t, rows, :] = mean_v
        return carry

    lax.fori_loop(first, end, tile, 0)


def inner_rows(
    own_ref, ea_ref, eb_ref, ft_ref, fv_ref,
    u_all, v_all, p_all, u_new, v_new, u_next, v_next, sums, later_sums, bed, start, flows, height_in, later,
    flat, flow_u, flow_v, height,
):
    even_lon = lax.rem(lax.axis_index("lon"), 2) == 0
    place = [u_all.at[k] for k in range(LEVELS)] + [v_all.at[k] for k in range(LEVELS)]
    place += [p_all.at[k] for k in range(LEVELS)] + [flat.at[BED], flat.at[FROM], height]
    for pack in range(PACKS):
        for at in range(0, ROWS, 32):
            a, b = ea_ref[pack, pl.ds(at, 32), :], eb_ref[pack, pl.ds(at, 32), :]
            east, west = jnp.where(even_lon, a, b), jnp.where(even_lon, b, a)
            tiles = [beside(east, west, p) for p in planes_of(pack)]
            for p, tile in zip(planes_of(pack), tiles):
                place[p][0, pl.ds(PAD + OWN + at, 32), :] = own_ref[p, pl.ds(at, 32), :]
                place[p][1, pl.ds(PAD + OWN + at, 32), :] = tile
    faces(OWN, 48, flat, ft_ref, fv_ref, False)
    faces(OWN + 48, 40, flat, ft_ref, fv_ref, False)

    def first(r, carry):
        mask_rows(r, flat, u_all, v_all, flow_u, flow_v)
        return carry

    def second(r, carry):
        tendencies(r, flat, ft_ref, fv_ref, u_all, v_all, p_all, u_new, v_new)
        return carry

    lax.fori_loop(INNER[0] - 1, INNER[1] + 1, first, 0)
    lax.fori_loop(INNER[0], INNER[1], second, 0)
    own = pl.ds(PAD + OWN, ROWS)
    inner = pl.ds(PAD + 8 * INNER[0], 8 * (INNER[1] - INNER[0]))
    masked = pl.ds(PAD + 8 * (INNER[0] - 1), 8 * (INNER[1] - INNER[0] + 2))
    core = pl.ds(PAD + CORE_ROWS[0], CORE_ROWS[1])
    for t in range(2):
        bed[t, own, :] = flat[BED, t, own, :]
        start[t, own, :] = flat[FROM, t, own, :]
        height_in[t, own, :] = height[t, own, :]
        flows[0, t, masked, :] = flow_u[0, t, masked, :]
        flows[1, t, masked, :] = flow_v[0, t, masked, :]
        for i, which in enumerate(SUMS):
            sums[i, t, inner, :] = flat[which, t, inner, :]
        for flow in (flow_u, flow_v):
            flow[1, t, pl.ds(PAD + 8 * INNER[0] - 8, 8), :] = jnp.zeros((8, LANES), jnp.float32)
            flow[1, t, pl.ds(PAD + 8 * INNER[1], 8), :] = jnp.zeros((8, LANES), jnp.float32)
    substeps(INNER_CHUNKS, None, flat, flow_u, flow_v, height)
    correct(INNER[0], INNER[1], flat, u_new, v_new, u_next, v_next, flow_u, flow_v)

    def third(r, carry):
        tendencies(r, flat, ft_ref, fv_ref, u_next, v_next, p_all, u_new, v_new)
        return carry

    lax.fori_loop(CORE[0], CORE[1], third, 0)
    for t in range(2):
        later[0, t, core, :] = flow_u[0, t, core, :]
        later[1, t, core, :] = flow_v[0, t, core, :]
        later[2, t, core, :] = height[t, core, :]
        for i, which in enumerate(SUMS):
            later_sums[i, t, core, :] = flat[which, t, core, :]


def ocean_steps(
    na_ref, nb_ref, ft_ref, fv_ref,
    u_in, v_in, p_in, u_done, v_done, u_next, v_next, sums, later_sums, bed, start, flows, height_in, later,
    u_out, v_out, h_out,
    u_all, v_all, p_all, u_new, v_new,
    flat, flow_u, flow_v, height,
):
    lat = lax.axis_index("lat")
    even_lat = lax.rem(lat, 2) == 0
    even_lon = lax.rem(lax.axis_index("lon"), 2) == 0
    top = lat == lax.axis_size("lat") - 1
    place = [u_all.at[k] for k in range(LEVELS)] + [v_all.at[k] for k in range(LEVELS)]
    place += [p_all.at[k] for k in range(LEVELS)] + [flat.at[BED], flat.at[FROM], height]

    def north_rows(p):
        return jnp.where(even_lat, na_ref[pl.ds(p * HALO, HALO), :], nb_ref[pl.ds(p * FOLD, HALO), :])

    def south_rows(p):
        return jnp.where(even_lat, nb_ref[pl.ds(p * FOLD + FOLD - HALO, HALO), :], na_ref[pl.ds(p * HALO, HALO), :])

    own = pl.ds(PAD + OWN, ROWS)
    low = pl.ds(PAD + OWN, 8 * (CORE[0] + 1) - OWN)
    high = pl.ds(PAD + 8 * (CORE[1] - 1), OWN + ROWS - 8 * (CORE[1] - 1))
    core = pl.ds(PAD + CORE_ROWS[0], CORE_ROWS[1])
    inner = pl.ds(PAD + 8 * INNER[0], 8 * (INNER[1] - INNER[0]))
    masked = pl.ds(PAD + 8 * (INNER[0] - 1), 8 * (INNER[1] - INNER[0] + 2))
    for t in range(2):
        for k in range(LEVELS):
            for rows in (low, high):
                p_all[k, t, rows, :] = p_in[k, t, rows, :]
                u_all[k, t, rows, :] = u_in[k, t, rows, :]
                v_all[k, t, rows, :] = v_in[k, t, rows, :]
        flat[BED, t, own, :] = bed[t, own, :]
        flat[FROM, t, own, :] = start[t, own, :]
        height[t, own, :] = height_in[t, own, :]
        flow_u[0, t, masked, :] = flows[0, t, masked, :]
        flow_v[0, t, masked, :] = flows[1, t, masked, :]
        for i, which in enumerate(SUMS):
            flat[which, t, inner, :] = sums[i, t, inner, :]
            flat[which, t, pl.ds(PAD + EXT - 8, 8), :] = jnp.zeros((8, LANES), jnp.float32)

    edge, after = pl.ds(0, PAD), pl.ds(PAD + OWN + ROWS + HALO, 16)
    for pack in range(PACKS):
        pa, pb = PLANES + pack, PLANES + PACKS + pack
        for rows, at in ((south_rows, PAD), (north_rows, PAD + OWN + ROWS)):
            a, b = rows(pa), rows(pb)
            east, west = jnp.where(even_lon, a, b), jnp.where(even_lon, b, a)
            tiles = [(rows(p), beside(east, west, p)) for p in planes_of(pack)]
            for p, (t0, t1) in zip(planes_of(pack), tiles):
                place[p][0, pl.ds(at, HALO), :] = t0
                place[p][1, pl.ds(at, HALO), :] = t1
        for p in planes_of(pack):
            for t in range(2):
                place[p][t, edge, :] = jnp.full((PAD, LANES), beyond(p), jnp.float32)
                place[p][t, after, :] = jnp.full((16, LANES), beyond(p), jnp.float32)

    @pl.when(top)
    def _():
        lane = lanes_of((24, LANES))

        def flipped(x):
            return jnp.take_along_axis(x, LANES - 1 - lane, axis=1)

        for pack in range(PACKS):
            a = flipped(nb_ref[pl.ds((PLANES + pack) * FOLD, 24), :])
            b = flipped(nb_ref[pl.ds((PLANES + PACKS + pack) * FOLD, 24), :])
            east, west = jnp.where(even_lon, b, a), jnp.where(even_lon, a, b)
            tiles = []
            for p in planes_of(pack):
                slot = HALO * (p % 8)
                e = pltpu.roll(west, (slot + HALO) % LANES, 1) if slot != LANES - HALO else west
                w = pltpu.roll(east, slot, 1) if slot else east
                t0 = flipped(nb_ref[pl.ds(p * FOLD, 24), :])
                t1 = jnp.where(lane < HALO, e, jnp.where(lane >= LANES - HALO, w, beyond(p)))
                if p < LEVELS:
                    t0, t1 = eastward(t0, t1)
                    t0, t1 = -t0, -t1
                tiles.append((t0, t1))
            for p, (t0, t1) in zip(planes_of(pack), tiles):
                place[p][0, pl.ds(PAD + PATCH, FOLD), :] = t0[:FOLD]
                place[p][1, pl.ds(PAD + PATCH, FOLD), :] = t1[:FOLD]

    fold_ghosts(flat.at[BED], top)
    for at, n in CHUNKS:
        faces(at, n, flat, ft_ref, fv_ref, top)
    for flow in (flow_u, flow_v):
        for now in range(2):
            for t in range(2):
                flow[now, t, edge, :] = jnp.zeros((PAD, LANES), jnp.float32)
                flow[now, t, pl.ds(PAD + EXT, PAD), :] = jnp.zeros((PAD, LANES), jnp.float32)

    def mask_first(r, carry):
        mask_rows(r, flat, u_all, v_all, flow_u, flow_v)
        return carry

    lax.fori_loop(0, INNER[0] - 1, mask_first, 0)
    lax.fori_loop(INNER[1] + 1, EXT // 8, mask_first, 0)

    def ghosts():
        for k in range(LEVELS):
            fold_ghosts(u_all.at[k], top)
            fold_ghosts(v_all.at[k], top, -1.0)
        fold_ghosts(flow_u.at[0], top)

    def tend(r, carry):
        tendencies(r, flat, ft_ref, fv_ref, u_all, v_all, p_all, u_new, v_new)
        return carry

    for k in range(LEVELS):
        fold_ghosts(p_all.at[k], top)
    ghosts()
    lax.fori_loop(0, INNER[0], tend, 0)
    lax.fori_loop(INNER[1], jnp.where(top, EXT // 8, EXT // 8 - 1), tend, 0)
    for flow in (flow_u, flow_v):
        for t in range(2):
            for at in (40, 72):
                flow[1, t, pl.ds(PAD + at, 8), :] = jnp.zeros((8, LANES), jnp.float32)
    substeps(OUTER_CHUNKS, top, flat, flow_u, flow_v, height)
    correct(0, INNER[0], flat, u_new, v_new, u_all, v_all, flow_u, flow_v)
    correct(INNER[0], CORE[0], flat, u_done, v_done, u_all, v_all, flow_u, flow_v)
    correct(CORE[1], INNER[1], flat, u_done, v_done, u_all, v_all, flow_u, flow_v)
    correct(INNER[1], EXT // 8, flat, u_new, v_new, u_all, v_all, flow_u, flow_v)

    for t in range(2):
        for k in range(LEVELS):
            for at in (8 * CORE[0], 8 * CORE[1] - 8):
                rows = pl.ds(PAD + at, 8)
                u_all[k, t, rows, :] = u_next[k, t, rows, :]
                v_all[k, t, rows, :] = v_next[k, t, rows, :]
        flow_u[0, t, core, :] = later[0, t, core, :]
        flow_v[0, t, core, :] = later[1, t, core, :]
        height[t, core, :] = later[2, t, core, :]
        for i, which in enumerate(SUMS):
            flat[which, t, core, :] = later_sums[i, t, core, :]
    ghosts()
    lax.fori_loop(1, CORE[0], tend, 0)
    lax.fori_loop(CORE[1], jnp.where(top, EXT // 8, EXT // 8 - 2), tend, 0)
    substeps(CHUNKS, top, flat, flow_u, flow_v, height)
    correct(OWN // 8, CORE[0], flat, u_new, v_new, u_out, v_out, None, None)
    correct(CORE[0], CORE[1], flat, u_done, v_done, u_out, v_out, None, None)
    correct(CORE[1], (OWN + ROWS) // 8, flat, u_new, v_new, u_out, v_out, None, None)
    h_out[...] = height[0, pl.ds(PAD + OWN, ROWS), :]


def lon_swaps():
    count = lax.axis_size("lon")
    first = [(i, i ^ 1) for i in range(count)]
    second = [(i, (((i + 1) % count) ^ 1) - 1) for i in range(count)]
    return first, [(i, j % count) for i, j in second]


def lat_swaps():
    lats, lons = lax.axis_size("lat"), lax.axis_size("lon")
    first, second = [], []
    for lat in range(lats):
        for lon in range(lons):
            first.append((lon * lats + lat, lon * lats + (lat ^ 1)))
            if lat == lats - 1:
                second.append((lon * lats + lat, (lons - 1 - lon) * lats + lat))
            elif lat:
                second.append((lon * lats + lat, lon * lats + ((lat + 1) ^ 1) - 1))
    return first, second


def turning(lat):
    lats = lax.axis_size("lat")
    ext = jnp.arange(TALL, dtype=jnp.int32) - PAD
    mirror = (lat == lats - 1) & (ext >= PATCH)
    row = jnp.where(mirror, lats * ROWS - FOLD + ext - PATCH, lat * ROWS + ext - OWN).astype(jnp.float32)
    sign = jnp.where(mirror, -0.25 * coriolis, 0.25 * coriolis)
    cells = lats * ROWS
    centre = sign * jnp.sin(math.pi * ((row + 0.5) / cells - 0.5))
    face = sign * jnp.sin(math.pi * ((row + 1.0) / cells - 0.5))
    wide = (TALL, LANES)
    return jnp.broadcast_to(centre[:, None], wide), jnp.broadcast_to(face[:, None], wide)


def whole(*shape):
    return pl.BlockSpec(shape, lambda *_: (0,) * len(shape))


def shards(u_velocity, v_velocity, density, surface, land_mask, bottom):
    f32 = jnp.float32
    params = pltpu.CompilerParams(vmem_limit_bytes=VMEM_LIMIT)
    level_block = (LEVELS, ROWS, LANES)
    fields = (u_velocity, v_velocity, density, surface, land_mask, bottom)
    pack_a, pack_b = pl.pallas_call(
        strips,
        out_shape=(jax.ShapeDtypeStruct((PACKS, ROWS, LANES), f32),) * 2,
        in_specs=[pl.BlockSpec(memory_space=pltpu.HBM)] * 6,
        scratch_shapes=[pltpu.VMEM(level_block, f32)] * 3
        + [pltpu.VMEM((ROWS, LANES), f32), pltpu.VMEM(level_block, jnp.int32), pltpu.VMEM((ROWS, LANES), jnp.int32)]
        + [pltpu.SemaphoreType.DMA((6,))],
        compiler_params=pltpu.CompilerParams(vmem_limit_bytes=56 * 1024 * 1024),
    )(*fields)
    lon_first, lon_second = lon_swaps()
    east_a = lax.ppermute(pack_a, "lon", lon_first)
    east_b = lax.ppermute(pack_b, "lon", lon_second)
    own = pl.pallas_call(
        own_block,
        out_shape=jax.ShapeDtypeStruct((PLANES, ROWS, LANES), f32),
        compiler_params=pltpu.CompilerParams(vmem_limit_bytes=8 * 1024 * 1024),
        cost_estimate=pl.CostEstimate(flops=4000000, bytes_accessed=5000000, transcendentals=0),
    )(*fields)

    low = lambda planes: pl.BlockSpec((planes, 24, LANES), lambda i: (0, 0, 0))
    high = lambda planes: pl.BlockSpec((planes, 24, LANES), lambda i: (0, ROWS // 24 - 1, 0))
    rows_a, rows_b = pl.pallas_call(
        outer_rows,
        grid=(1,),
        in_specs=[low(PLANES), low(PACKS), low(PACKS), high(PLANES), high(PACKS), high(PACKS)],
        out_specs=(whole(SENT * HALO, LANES), whole(888, LANES)),
        out_shape=(
            jax.ShapeDtypeStruct((SENT * HALO, LANES), f32),
            jax.ShapeDtypeStruct((888, LANES), f32),
        ),
        compiler_params=params,
    )(own, east_a, east_b, own, east_a, east_b)
    lat_first, lat_second = lat_swaps()
    north_b = lax.ppermute(rows_b, ("lon", "lat"), lat_second)
    north_a = lax.ppermute(rows_a, ("lon", "lat"), lat_first)

    turn_centre, turn_face = turning(lax.axis_index("lat"))
    levels, pair, single = (LEVELS, 2, TALL, LANES), (2, 2, TALL, LANES), (2, TALL, LANES)
    four, three = (4, 2, TALL, LANES), (3, 2, TALL, LANES)
    shapes = [levels] * 7 + [four, four, single, single, pair, single, three]
    done = pl.pallas_call(
        inner_rows,
        out_shape=tuple(jax.ShapeDtypeStruct(shape, f32) for shape in shapes),
        scratch_shapes=[pltpu.VMEM((16, 2, TALL, LANES), f32)]
        + [pltpu.VMEM(pair, f32), pltpu.VMEM(pair, f32), pltpu.VMEM(single, f32)],
        compiler_params=pltpu.CompilerParams(vmem_limit_bytes=12 * 1024 * 1024),
        cost_estimate=pl.CostEstimate(flops=40000000, bytes_accessed=12000000, transcendentals=0),
    )(own, east_a, east_b, turn_centre, turn_face)
    return pl.pallas_call(
        ocean_steps,
        out_shape=(
            jax.ShapeDtypeStruct(level_block, f32),
            jax.ShapeDtypeStruct(level_block, f32),
            jax.ShapeDtypeStruct((ROWS, LANES), f32),
        ),
        scratch_shapes=[pltpu.VMEM(levels, f32)] * 5
        + [pltpu.VMEM((16, 2, TALL, LANES), f32)]
        + [pltpu.VMEM(pair, f32), pltpu.VMEM(pair, f32), pltpu.VMEM(single, f32)],
        compiler_params=params,
    )(north_a, north_b, turn_centre, turn_face, *done)


def solution(mesh):
    return jax.shard_map(
        shards,
        mesh=mesh,
        in_specs=(
            P(None, "lat", "lon"),
            P(None, "lat", "lon"),
            P(None, "lat", "lon"),
            P("lat", "lon"),
            P(None, "lat", "lon"),
            P("lat", "lon"),
        ),
        out_specs=(P(None, "lat", "lon"), P(None, "lat", "lon"), P("lat", "lon")),
        check_vma=False,
    )
```

```python
import math

import jax
import jax.numpy as jnp
from jax import lax
from jax.experimental import pallas as pl
from jax.experimental.pallas import tpu as pltpu
from jax.sharding import PartitionSpec as P

SUBSTEPS = 8
STEPS = 2
LEVELS = 12
ROWS = 96
LANES = 128
HALO = 16
FOLD = 18

PLANES = 3 * LEVELS + 3
BOTTOM, FIRST, SURFACE = 36, 37, 38
PACKS = -(-PLANES // 8)
SENT = PLANES + 2 * PACKS

PAD = 8
EXT = 136
TALL = PAD + EXT + PAD
OWN = HALO
GHOST_A, PATCH, GHOST_B = OWN + ROWS, OWN + ROWS + 1, OWN + ROWS + 1 + FOLD
CHUNKS = ((0, 32), (32, 32), (64, 32), (96, 40))

viscosity = 0.05
friction = 0.1
coriolis = 0.25
substep_time = 0.4
layer = 1.0 / LEVELS
step_time = SUBSTEPS * substep_time
drag = 1.0 / (1.0 + step_time * friction)

VMEM_LIMIT = 24 * 1024 * 1024


def lanes_of(shape):
    return lax.broadcasted_iota(jnp.int32, shape, len(shape) - 1)


def masked_planes(u_ref, v_ref, d_ref, s_ref, m_ref, b_ref, ready):
    lane = lanes_of((ROWS, LANES))
    row = lax.broadcasted_iota(jnp.int32, (ROWS, LANES), 0)
    ready(5)
    ready(4)
    bottom = b_ref[...].astype(jnp.float32)
    first = bottom - jnp.sum(m_ref[...], axis=0).astype(jnp.float32)
    east = jnp.where(lane == LANES - 1, 12.0, pltpu.roll(bottom, LANES - 1, 1))
    north = jnp.where(row == ROWS - 1, 12.0, pltpu.roll(bottom, ROWS - 1, 0))
    up_u, up_v = jnp.minimum(bottom, east), jnp.minimum(bottom, north)
    ready(0)
    for k in range(LEVELS):
        yield k, jnp.where((first <= k) & (up_u > k), u_ref[k], 0.0)
    ready(1)
    for k in range(LEVELS):
        yield LEVELS + k, jnp.where((first <= k) & (up_v > k), v_ref[k], 0.0)
    ready(2)
    running = jnp.zeros_like(bottom)
    for k in range(LEVELS):
        weighted = jnp.where((first <= k) & (bottom > k), d_ref[k], 0.0)
        running = running + weighted
        yield 2 * LEVELS + k, layer * (running - 0.5 * weighted)
    ready(3)
    yield BOTTOM, bottom
    yield FIRST, first
    yield SURFACE, jnp.where(bottom > 0.0, s_ref[...], 0.0)


def strips(u_far, v_far, d_far, s_far, m_far, b_far, a_ref, c_ref, u_ref, v_ref, d_ref, s_ref, m_ref, b_ref, sems):
    pairs = ((u_far, u_ref), (v_far, v_ref), (d_far, d_ref), (s_far, s_ref), (m_far, m_ref), (b_far, b_ref))
    copies = [pltpu.make_async_copy(far, near, sems.at[i]) for i, (far, near) in enumerate(pairs)]
    for i in (5, 4, 0, 1, 2, 3):
        copies[i].start()
    lane = lanes_of((ROWS, LANES))
    even = lax.rem(lax.axis_index("lon"), 2) == 0
    for p, plane in masked_planes(u_ref, v_ref, d_ref, s_ref, m_ref, b_ref, lambda i: copies[i].wait()):
        slot = p % 8
        here = (lane >= HALO * slot) & (lane < HALO * slot + HALO)
        if slot == 0:
            to_east = to_west = jnp.zeros((ROWS, LANES), jnp.float32)
        to_east = jnp.where(here, pltpu.roll(plane, (HALO * slot + HALO) % LANES, 1), to_east)
        to_west = jnp.where(here, pltpu.roll(plane, HALO * slot, 1) if slot else plane, to_west)
        if slot == 7 or p == PLANES - 1:
            a_ref[p // 8] = jnp.where(even, to_east, to_west)
            c_ref[p // 8] = jnp.where(even, to_west, to_east)


def own_block(u_ref, v_ref, d_ref, s_ref, m_ref, b_ref, own_ref):
    for p, plane in masked_planes(u_ref, v_ref, d_ref, s_ref, m_ref, b_ref, lambda i: None):
        own_ref[p] = plane


def outer_rows(low_own, low_a, low_b, top_own, top_a, top_b, a_ref, c_ref):
    even = lax.rem(lax.axis_index("lat"), 2) == 0
    for p in range(SENT):
        if p < PLANES:
            low, top = low_own[p], top_own[p]
        elif p < PLANES + PACKS:
            low, top = low_a[p - PLANES], top_a[p - PLANES]
        else:
            low, top = low_b[p - PLANES - PACKS], top_b[p - PLANES - PACKS]
        a_ref[pl.ds(p * HALO, HALO), :] = jnp.where(even, top[24 - HALO :], low[:HALO])
        c_ref[pl.ds(p * FOLD, FOLD), :] = jnp.where(even, low[:FOLD], top[24 - FOLD :])


def eastward(t0, t1):
    lane = lanes_of(t0.shape)
    r0, r1 = pltpu.roll(t0, LANES - 1, t0.ndim - 1), pltpu.roll(t1, LANES - 1, t0.ndim - 1)
    edge = lane == LANES - 1
    return jnp.where(edge, r1, r0), jnp.where(edge, r0, r1)


def westward(t0, t1):
    lane = lanes_of(t0.shape)
    r0, r1 = pltpu.roll(t0, 1, t0.ndim - 1), pltpu.roll(t1, 1, t0.ndim - 1)
    edge = lane == 0
    return jnp.where(edge, r1, r0), jnp.where(edge, r0, r1)


def fold_ghosts(ref, top, sign=1.0):
    for t in range(2):
        for ghost, source in ((GHOST_A, PATCH + FOLD - 2), (GHOST_B, OWN + ROWS - 2)):
            kept = ref[t, pl.ds(PAD + ghost, 1), :]
            taken = ref[t, pl.ds(PAD + source, 1), :]
            ref[t, pl.ds(PAD + ghost, 1), :] = jnp.where(top, sign * taken, kept)


(BED, FROM, UP_U, LO_U, UP_V, C_U, F_U, G_U, C_V, F_V, G_V, SUM_U, SUM_V, NEW_U, NEW_V, SEA) = range(16)
INNER = (3, 12)
CORE = (4, 11)
CORE_ROWS = 88
SUMS = (G_U, G_V, NEW_U, NEW_V)


def beyond(p):
    return 12.0 if p in (BOTTOM, FIRST) else 0.0


def beside(east, west, p):
    lane = lanes_of(east.shape)
    slot = HALO * (p % 8)
    e = pltpu.roll(east, LANES - slot, 1) if slot else east
    w = pltpu.roll(west, (2 * LANES - HALO - slot) % LANES, 1) if slot != LANES - HALO else west
    return jnp.where(lane < HALO, e, jnp.where(lane >= LANES - HALO, w, beyond(p)))


def planes_of(pack):
    return range(8 * pack, min(8 * pack + 8, PLANES))


def faces(at, n, flat, ft_ref, fv_ref, top):
    rows, up = pl.ds(PAD + at, n), pl.ds(PAD + at + 1, n)
    bed = [flat[BED, t, rows, :] for t in range(2)]
    start = [flat[FROM, t, rows, :] for t in range(2)]
    bed_east = eastward(*bed)
    start_east = eastward(*start)
    ext_row = lax.broadcasted_iota(jnp.int32, (n, LANES), 0) + at
    mirror = (ext_row >= jnp.where(top, PATCH, EXT)) & (ext_row < PATCH + FOLD)
    for t in range(2):
        up_u = jnp.minimum(bed[t], bed_east[t])
        lo_u = jnp.where(mirror, start_east[t], start[t])
        up_v = jnp.minimum(bed[t], flat[BED, t, up, :])
        count_u = jnp.maximum(up_u - lo_u, 0.0)
        count_v = jnp.maximum(up_v - start[t], 0.0)
        flat[UP_U, t, rows, :] = up_u
        flat[LO_U, t, rows, :] = lo_u
        flat[UP_V, t, rows, :] = up_v
        flat[C_U, t, rows, :] = count_u * (-substep_time * layer)
        flat[C_V, t, rows, :] = count_v * (-substep_time * layer)
        flat[F_U, t, rows, :] = jnp.where(count_u > 0.0, substep_time * ft_ref[rows, :], 0.0)
        flat[F_V, t, rows, :] = jnp.where(count_v > 0.0, -substep_time * fv_ref[rows, :], 0.0)
        flat[SEA, t, rows, :] = jnp.where(bed[t] > 0.0, substep_time, 0.0)


def mask_rows(r, flat, u_all, v_all, flow_u, flow_v):
    rows = pl.ds(pl.multiple_of(r * 8, 8) + PAD, 8)
    for t in range(2):
        lo_u, up_u = flat[LO_U, t, rows, :], flat[UP_U, t, rows, :]
        lo_v, up_v = flat[FROM, t, rows, :], flat[UP_V, t, rows, :]
        us = [jnp.where((lo_u <= k) & (up_u > k), u_all[k, t, rows, :], 0.0) for k in range(LEVELS)]
        vs = [jnp.where((lo_v <= k) & (up_v > k), v_all[k, t, rows, :], 0.0) for k in range(LEVELS)]
        for k in range(LEVELS):
            u_all[k, t, rows, :] = us[k]
            v_all[k, t, rows, :] = vs[k]
        flow_u[0, t, rows, :] = layer * sum(us[1:], us[0])
        flow_v[0, t, rows, :] = layer * sum(vs[1:], vs[0])


def tendencies(r, flat, ft_ref, fv_ref, u_all, v_all, p_all, u_new, v_new):
    base = pl.multiple_of(r * 8, 8) + PAD
    rows, up, down = pl.ds(base, 8), pl.ds(base + 1, 8), pl.ds(base - 1, 8)
    ft, fv = ft_ref[rows, :], fv_ref[rows, :]
    lo_u = [flat[LO_U, t, rows, :] for t in range(2)]
    up_u = [flat[UP_U, t, rows, :] for t in range(2)]
    lo_v = [flat[FROM, t, rows, :] for t in range(2)]
    up_v = [flat[UP_V, t, rows, :] for t in range(2)]
    zero = jnp.zeros((8, LANES), jnp.float32)
    force_u, force_v, total_u, total_v = [zero] * 2, [zero] * 2, [zero] * 2, [zero] * 2
    for k in range(LEVELS):
        eu, wu, ru, ev, wv, rv, u0s, v0s = [], [], [], [], [], [], [], []
        for t in range(2):
            u0, un, us = u_all[k, t, rows, :], u_all[k, t, up, :], u_all[k, t, down, :]
            v0, vn, vs = v_all[k, t, rows, :], v_all[k, t, up, :], v_all[k, t, down, :]
            p0, pn = p_all[k, t, rows, :], p_all[k, t, up, :]
            turn_v = ft * (v0 + vs)
            turn_u = fv * (u0 + un)
            a = viscosity * u0
            c = viscosity * v0
            eu.append(a - p0 + turn_v)
            wu.append(a)
            ru.append(viscosity * (un + us) - 4.0 * a + p0 + turn_v)
            ev.append(c)
            wv.append(c - turn_u)
            rv.append(viscosity * (vn + vs) - 4.0 * c + (p0 - pn) - turn_u)
            u0s.append(u0)
            v0s.append(v0)
        eu, wu, ev, wv = eastward(*eu), westward(*wu), eastward(*ev), westward(*wv)
        for t in range(2):
            tend_u = jnp.where((lo_u[t] <= k) & (up_u[t] > k), eu[t] + wu[t] + ru[t], 0.0)
            tend_v = jnp.where((lo_v[t] <= k) & (up_v[t] > k), ev[t] + wv[t] + rv[t], 0.0)
            force_u[t] = force_u[t] + tend_u
            force_v[t] = force_v[t] + tend_v
            new_u = u0s[t] + step_time * tend_u
            new_v = v0s[t] + step_time * tend_v
            new_u = jnp.where(up_u[t] == k + 1, drag * new_u, new_u)
            new_v = jnp.where(up_v[t] == k + 1, drag * new_v, new_v)
            total_u[t] = total_u[t] + new_u
            total_v[t] = total_v[t] + new_v
            u_new[k, t, rows, :] = new_u
            v_new[k, t, rows, :] = new_v
    for t in range(2):
        flat[G_U, t, rows, :] = (substep_time * layer) * force_u[t]
        flat[G_V, t, rows, :] = (substep_time * layer) * force_v[t]
        flat[NEW_U, t, rows, :] = layer * total_u[t]
        flat[NEW_V, t, rows, :] = layer * total_v[t]


def substep(now, later, chunks, top, flat, flow_u, flow_v, height):
    for at, n in chunks:
        rows, down = pl.ds(PAD + at, n), pl.ds(PAD + at - 1, n)
        u = [flow_u[now, t, rows, :] for t in range(2)]
        uw = westward(*u)
        for t in range(2):
            spread = u[t] - uw[t] + flow_v[now, t, rows, :] - flow_v[now, t, down, :]
            height[t, rows, :] = height[t, rows, :] - flat[SEA, t, rows, :] * spread
    if top is not None:
        fold_ghosts(height, top)
    for at, n in chunks:
        rows, up, down = pl.ds(PAD + at, n), pl.ds(PAD + at + 1, n), pl.ds(PAD + at - 1, n)
        h = [height[t, rows, :] for t in range(2)]
        he = eastward(*h)
        qv = [flow_v[now, t, rows, :] + flow_v[now, t, down, :] for t in range(2)]
        qve = eastward(*qv)
        qu = [flow_u[now, t, rows, :] + flow_u[now, t, up, :] for t in range(2)]
        quw = westward(*qu)
        for t in range(2):
            next_u = (
                flow_u[now, t, rows, :]
                + flat[C_U, t, rows, :] * (he[t] - h[t])
                + flat[F_U, t, rows, :] * (qv[t] + qve[t])
                + flat[G_U, t, rows, :]
            )
            next_v = (
                flow_v[now, t, rows, :]
                + flat[C_V, t, rows, :] * (height[t, up, :] - h[t])
                + flat[F_V, t, rows, :] * (qu[t] + quw[t])
                + flat[G_V, t, rows, :]
            )
            flow_u[later, t, rows, :] = next_u
            flow_v[later, t, rows, :] = next_v
            flat[SUM_U, t, rows, :] = flat[SUM_U, t, rows, :] + next_u
            flat[SUM_V, t, rows, :] = flat[SUM_V, t, rows, :] + next_v
    if top is not None:
        fold_ghosts(flow_u.at[later], top)


def substeps(chunks, top, flat, flow_u, flow_v, height):
    for which in (SUM_U, SUM_V):
        for t in range(2):
            flat[which, t, pl.ds(PAD, EXT), :] = jnp.zeros((EXT, LANES), jnp.float32)

    def two(turn, carry):
        substep(0, 1, chunks, top, flat, flow_u, flow_v, height)
        substep(1, 0, chunks, top, flat, flow_u, flow_v, height)
        return carry

    lax.fori_loop(0, SUBSTEPS // 2, two, 0)


def correct(first, end, flat, u_from, v_from, u_to, v_to, flow_u, flow_v):
    def tile(r, carry):
        rows = pl.ds(pl.multiple_of(r * 8, 8) + PAD, 8)
        last = flow_u is None
        for t in range(1 if last else 2):
            lo_u, up_u = flat[LO_U, t, rows, :], flat[UP_U, t, rows, :]
            lo_v, up_v = flat[FROM, t, rows, :], flat[UP_V, t, rows, :]
            mean_u = flat[SUM_U, t, rows, :] / SUBSTEPS
            mean_v = flat[SUM_V, t, rows, :] / SUBSTEPS
            depth_u = layer * jnp.maximum(up_u - lo_u, 1.0)
            depth_v = layer * jnp.maximum(up_v - lo_v, 1.0)
            add_u = (mean_u - flat[NEW_U, t, rows, :]) / depth_u
            add_v = (mean_v - flat[NEW_V, t, rows, :]) / depth_v
            us = [jnp.where((lo_u <= k) & (up_u > k), u_from[k, t, rows, :] + add_u, 0.0) for k in range(LEVELS)]
            vs = [jnp.where((lo_v <= k) & (up_v > k), v_from[k, t, rows, :] + add_v, 0.0) for k in range(LEVELS)]
            for k in range(LEVELS):
                if last:
                    out = pl.ds(pl.multiple_of(r * 8 - OWN, 8), 8)
                    u_to[k, out, :] = us[k]
                    v_to[k, out, :] = vs[k]
                else:
                    u_to[k, t, rows, :] = us[k]
                    v_to[k, t, rows, :] = vs[k]
            if not last:
                flow_u[0, t, rows, :] = mean_u
                flow_v[0, t, rows, :] = mean_v
        return carry

    lax.fori_loop(first, end, tile, 0)


def inner_rows(
    own_ref, ea_ref, eb_ref, na_ref, ft_ref, fv_ref,
    u_all, v_all, p_all, u_new, v_new, u_next, v_next, sums, later_sums, bed, start, flows, height_in, later,
    flat, flow_u, flow_v, height,
):
    even_lat = lax.rem(lax.axis_index("lat"), 2) == 0
    even_lon = lax.rem(lax.axis_index("lon"), 2) == 0
    place = [u_all.at[k] for k in range(LEVELS)] + [v_all.at[k] for k in range(LEVELS)]
    place += [p_all.at[k] for k in range(LEVELS)] + [flat.at[BED], flat.at[FROM], height]
    for pack in range(PACKS):
        for at in range(0, ROWS, 32):
            a, b = ea_ref[pack, pl.ds(at, 32), :], eb_ref[pack, pl.ds(at, 32), :]
            east, west = jnp.where(even_lon, a, b), jnp.where(even_lon, b, a)
            tiles = [beside(east, west, p) for p in planes_of(pack)]
            for p, tile in zip(planes_of(pack), tiles):
                place[p][0, pl.ds(PAD + OWN + at, 32), :] = own_ref[p, pl.ds(at, 32), :]
                place[p][1, pl.ds(PAD + OWN + at, 32), :] = tile
        at = pl.multiple_of(jnp.where(even_lat, PAD + OWN + ROWS, PAD), 8)
        a, b = na_ref[pl.ds((PLANES + pack) * HALO, HALO), :], na_ref[pl.ds((PLANES + PACKS + pack) * HALO, HALO), :]
        east, west = jnp.where(even_lon, a, b), jnp.where(even_lon, b, a)
        tiles = [(na_ref[pl.ds(p * HALO, HALO), :], beside(east, west, p)) for p in planes_of(pack)]
        for p, (t0, t1) in zip(planes_of(pack), tiles):
            place[p][0, pl.ds(at, HALO), :] = t0
            place[p][1, pl.ds(at, HALO), :] = t1
            for t in range(2):
                place[p][t, pl.ds(0, PAD), :] = jnp.full((PAD, LANES), beyond(p), jnp.float32)
                place[p][t, pl.ds(TALL - 16, 16), :] = jnp.full((16, LANES), beyond(p), jnp.float32)
    for at, n in CHUNKS:
        faces(at, n, flat, ft_ref, fv_ref, False)
    for t in range(2):
        for flow in (flow_u, flow_v):
            for now in range(2):
                flow[now, t, :, :] = jnp.zeros((TALL, LANES), jnp.float32)
        for which in (G_U, G_V):
            flat[which, t, pl.ds(PAD, EXT), :] = jnp.zeros((EXT, LANES), jnp.float32)

    def first(r, carry):
        mask_rows(r, flat, u_all, v_all, flow_u, flow_v)
        return carry

    def second(r, carry):
        tendencies(r, flat, ft_ref, fv_ref, u_all, v_all, p_all, u_new, v_new)
        return carry

    tiles = EXT // 8
    lax.fori_loop(jnp.where(even_lat, INNER[0] - 1, 0), jnp.where(even_lat, tiles, INNER[1] + 1), first, 0)
    begin, end = jnp.where(even_lat, INNER[0], 0), jnp.where(even_lat, tiles - 1, INNER[1])
    lax.fori_loop(begin, end, second, 0)
    own = pl.ds(PAD + OWN, ROWS)
    inner = pl.ds(PAD + 8 * INNER[0], 8 * (INNER[1] - INNER[0]))
    masked = pl.ds(PAD + 8 * (INNER[0] - 1), 8 * (INNER[1] - INNER[0] + 2))
    core = pl.ds(pl.multiple_of(jnp.where(even_lat, PAD + 8 * CORE[0], PAD), 8), CORE_ROWS)
    for t in range(2):
        bed[t, :, :] = flat[BED, t, :, :]
        start[t, :, :] = flat[FROM, t, :, :]
        height_in[t, own, :] = height[t, own, :]
        flows[0, t, masked, :] = flow_u[0, t, masked, :]
        flows[1, t, masked, :] = flow_v[0, t, masked, :]
        for i, which in enumerate(SUMS):
            sums[i, t, inner, :] = flat[which, t, inner, :]
    base = pl.multiple_of(8 * begin, 8)
    substeps(((base, 32), (base + 32, 32), (base + 64, 40)), None, flat, flow_u, flow_v, height)
    correct(begin, end, flat, u_new, v_new, u_next, v_next, flow_u, flow_v)

    def third(r, carry):
        tendencies(r, flat, ft_ref, fv_ref, u_next, v_next, p_all, u_new, v_new)
        return carry

    lax.fori_loop(jnp.where(even_lat, CORE[0], 1), jnp.where(even_lat, tiles - 2, CORE[1]), third, 0)
    for t in range(2):
        later[0, t, core, :] = flow_u[0, t, core, :]
        later[1, t, core, :] = flow_v[0, t, core, :]
        later[2, t, core, :] = height[t, core, :]
        for i, which in enumerate(SUMS):
            later_sums[i, t, core, :] = flat[which, t, core, :]


def ocean_steps(
    nb_ref, ft_ref, fv_ref,
    u_in, v_in, p_in, u_done, v_done, u_next, v_next, sums, later_sums, bed, start, flows, height_in, later,
    u_out, v_out, h_out,
    u_all, v_all, p_all, u_new, v_new,
    flat, flow_u, flow_v, height,
):
    lat = lax.axis_index("lat")
    even_lat = lax.rem(lat, 2) == 0
    even_lon = lax.rem(lax.axis_index("lon"), 2) == 0
    top = lat == lax.axis_size("lat") - 1
    place = [u_all.at[k] for k in range(LEVELS)] + [v_all.at[k] for k in range(LEVELS)]
    place += [p_all.at[k] for k in range(LEVELS)] + [flat.at[BED], flat.at[FROM], height]

    own = pl.ds(PAD + OWN, ROWS)
    low = pl.ds(PAD + OWN, 8 * (CORE[0] + 1) - OWN)
    high = pl.ds(PAD + 8 * (CORE[1] - 1), OWN + ROWS - 8 * (CORE[1] - 1))
    core = pl.ds(pl.multiple_of(jnp.where(even_lat, PAD + 8 * CORE[0], PAD), 8), CORE_ROWS)
    inner = pl.ds(PAD + 8 * INNER[0], 8 * (INNER[1] - INNER[0]))
    masked = pl.ds(PAD + 8 * (INNER[0] - 1), 8 * (INNER[1] - INNER[0] + 2))
    for t in range(2):
        for k in range(LEVELS):
            for rows in (low, high):
                p_all[k, t, rows, :] = p_in[k, t, rows, :]
                u_all[k, t, rows, :] = u_in[k, t, rows, :]
                v_all[k, t, rows, :] = v_in[k, t, rows, :]
        flat[BED, t, :, :] = bed[t, :, :]
        flat[FROM, t, :, :] = start[t, :, :]
        for flow in (flow_u, flow_v):
            for now in range(2):
                flow[now, t, :, :] = jnp.zeros((TALL, LANES), jnp.float32)
        height[t, own, :] = height_in[t, own, :]
        flow_u[0, t, masked, :] = flows[0, t, masked, :]
        flow_v[0, t, masked, :] = flows[1, t, masked, :]
        for i, which in enumerate(SUMS):
            flat[which, t, inner, :] = sums[i, t, inner, :]
            flat[which, t, pl.ds(PAD + EXT - 8, 8), :] = jnp.zeros((8, LANES), jnp.float32)

    edge, after = pl.ds(0, PAD), pl.ds(PAD + OWN + ROWS + HALO, 16)
    at = pl.multiple_of(jnp.where(even_lat, PAD, PAD + OWN + ROWS), 8)

    def rows_of(p):
        return jnp.where(even_lat, nb_ref[pl.ds(p * FOLD + FOLD - HALO, HALO), :], nb_ref[pl.ds(p * FOLD, HALO), :])

    for pack in range(PACKS):
        a, b = rows_of(PLANES + pack), rows_of(PLANES + PACKS + pack)
        east, west = jnp.where(even_lon, a, b), jnp.where(even_lon, b, a)
        tiles = [(rows_of(p), beside(east, west, p)) for p in planes_of(pack)]
        for p, (t0, t1) in zip(planes_of(pack), tiles):
            place[p][0, pl.ds(at, HALO), :] = t0
            place[p][1, pl.ds(at, HALO), :] = t1
        for p in planes_of(pack):
            for t in range(2):
                place[p][t, edge, :] = jnp.full((PAD, LANES), beyond(p), jnp.float32)
                place[p][t, after, :] = jnp.full((16, LANES), beyond(p), jnp.float32)

    @pl.when(top)
    def _():
        lane = lanes_of((24, LANES))

        def flipped(x):
            return jnp.take_along_axis(x, LANES - 1 - lane, axis=1)

        for pack in range(PACKS):
            a = flipped(nb_ref[pl.ds((PLANES + pack) * FOLD, 24), :])
            b = flipped(nb_ref[pl.ds((PLANES + PACKS + pack) * FOLD, 24), :])
            east, west = jnp.where(even_lon, b, a), jnp.where(even_lon, a, b)
            tiles = []
            for p in planes_of(pack):
                slot = HALO * (p % 8)
                e = pltpu.roll(west, (slot + HALO) % LANES, 1) if slot != LANES - HALO else west
                w = pltpu.roll(east, slot, 1) if slot else east
                t0 = flipped(nb_ref[pl.ds(p * FOLD, 24), :])
                t1 = jnp.where(lane < HALO, e, jnp.where(lane >= LANES - HALO, w, beyond(p)))
                if p < LEVELS:
                    t0, t1 = eastward(t0, t1)
                    t0, t1 = -t0, -t1
                tiles.append((t0, t1))
            for p, (t0, t1) in zip(planes_of(pack), tiles):
                place[p][0, pl.ds(PAD + PATCH, FOLD), :] = t0[:FOLD]
                place[p][1, pl.ds(PAD + PATCH, FOLD), :] = t1[:FOLD]

    fold_ghosts(flat.at[BED], top)
    for at, n in CHUNKS:
        faces(at, n, flat, ft_ref, fv_ref, top)
    def mask_first(r, carry):
        mask_rows(r, flat, u_all, v_all, flow_u, flow_v)
        return carry

    tiles = EXT // 8
    lax.fori_loop(jnp.where(even_lat, 0, INNER[1] + 1), jnp.where(even_lat, INNER[0] - 1, tiles), mask_first, 0)

    def ghosts():
        for k in range(LEVELS):
            fold_ghosts(u_all.at[k], top)
            fold_ghosts(v_all.at[k], top, -1.0)
        fold_ghosts(flow_u.at[0], top)

    def tend(r, carry):
        tendencies(r, flat, ft_ref, fv_ref, u_all, v_all, p_all, u_new, v_new)
        return carry

    for k in range(LEVELS):
        fold_ghosts(p_all.at[k], top)
    ghosts()
    first, end = jnp.where(even_lat, 0, INNER[1]), jnp.where(even_lat, INNER[0], jnp.where(top, tiles, tiles - 1))
    lax.fori_loop(first, end, tend, 0)
    base = pl.multiple_of(jnp.where(even_lat, 0, 8 * CORE[1] - 8), 8)
    substeps(((base, 24), (base + 24, 32)), top, flat, flow_u, flow_v, height)
    correct(first, jnp.where(even_lat, INNER[0], tiles), flat, u_new, v_new, u_all, v_all, flow_u, flow_v)
    between = jnp.where(even_lat, INNER[0], CORE[1])
    correct(between, between + 1, flat, u_done, v_done, u_all, v_all, flow_u, flow_v)

    for t in range(2):
        for k in range(LEVELS):
            for at in (8 * CORE[0], 8 * CORE[1] - 8):
                rows = pl.ds(PAD + at, 8)
                u_all[k, t, rows, :] = u_next[k, t, rows, :]
                v_all[k, t, rows, :] = v_next[k, t, rows, :]
        flow_u[0, t, core, :] = later[0, t, core, :]
        flow_v[0, t, core, :] = later[1, t, core, :]
        height[t, core, :] = later[2, t, core, :]
        for i, which in enumerate(SUMS):
            flat[which, t, core, :] = later_sums[i, t, core, :]
    ghosts()
    end = jnp.where(even_lat, CORE[0], jnp.where(top, tiles, tiles - 2))
    lax.fori_loop(jnp.where(even_lat, 1, CORE[1]), end, tend, 0)
    substeps(CHUNKS, top, flat, flow_u, flow_v, height)
    low, high = OWN // 8, (OWN + ROWS) // 8
    here = jnp.where(even_lat, low, CORE[1]), jnp.where(even_lat, CORE[0], high)
    done = jnp.where(even_lat, CORE[0], low), jnp.where(even_lat, high, CORE[1])
    correct(*here, flat, u_new, v_new, u_out, v_out, None, None)
    correct(*done, flat, u_done, v_done, u_out, v_out, None, None)
    h_out[...] = height[0, pl.ds(PAD + OWN, ROWS), :]


def lon_swaps():
    count = lax.axis_size("lon")
    first = [(i, i ^ 1) for i in range(count)]
    second = [(i, (((i + 1) % count) ^ 1) - 1) for i in range(count)]
    return first, [(i, j % count) for i, j in second]


def lat_swaps():
    lats, lons = lax.axis_size("lat"), lax.axis_size("lon")
    first, second = [], []
    for lat in range(lats):
        for lon in range(lons):
            first.append((lon * lats + lat, lon * lats + (lat ^ 1)))
            if lat == lats - 1:
                second.append((lon * lats + lat, (lons - 1 - lon) * lats + lat))
            elif lat:
                second.append((lon * lats + lat, lon * lats + ((lat + 1) ^ 1) - 1))
    return first, second


def turning(lat):
    lats = lax.axis_size("lat")
    ext = jnp.arange(TALL, dtype=jnp.int32) - PAD
    mirror = (lat == lats - 1) & (ext >= PATCH)
    row = jnp.where(mirror, lats * ROWS - FOLD + ext - PATCH, lat * ROWS + ext - OWN).astype(jnp.float32)
    sign = jnp.where(mirror, -0.25 * coriolis, 0.25 * coriolis)
    cells = lats * ROWS
    centre = sign * jnp.sin(math.pi * ((row + 0.5) / cells - 0.5))
    face = sign * jnp.sin(math.pi * ((row + 1.0) / cells - 0.5))
    wide = (TALL, LANES)
    return jnp.broadcast_to(centre[:, None], wide), jnp.broadcast_to(face[:, None], wide)


def whole(*shape):
    return pl.BlockSpec(shape, lambda *_: (0,) * len(shape))


def shards(u_velocity, v_velocity, density, surface, land_mask, bottom):
    f32 = jnp.float32
    params = pltpu.CompilerParams(vmem_limit_bytes=VMEM_LIMIT)
    level_block = (LEVELS, ROWS, LANES)
    fields = (u_velocity, v_velocity, density, surface, land_mask, bottom)
    pack_a, pack_b = pl.pallas_call(
        strips,
        out_shape=(jax.ShapeDtypeStruct((PACKS, ROWS, LANES), f32),) * 2,
        in_specs=[pl.BlockSpec(memory_space=pltpu.HBM)] * 6,
        scratch_shapes=[pltpu.VMEM(level_block, f32)] * 3
        + [pltpu.VMEM((ROWS, LANES), f32), pltpu.VMEM(level_block, jnp.int32), pltpu.VMEM((ROWS, LANES), jnp.int32)]
        + [pltpu.SemaphoreType.DMA((6,))],
        compiler_params=pltpu.CompilerParams(vmem_limit_bytes=56 * 1024 * 1024),
    )(*fields)
    lon_first, lon_second = lon_swaps()
    east_a = lax.ppermute(pack_a, "lon", lon_first)
    east_b = lax.ppermute(pack_b, "lon", lon_second)
    own = pl.pallas_call(
        own_block,
        out_shape=jax.ShapeDtypeStruct((PLANES, ROWS, LANES), f32),
        compiler_params=pltpu.CompilerParams(vmem_limit_bytes=8 * 1024 * 1024),
        cost_estimate=pl.CostEstimate(flops=4000000, bytes_accessed=5000000, transcendentals=0),
    )(*fields)

    low = lambda planes: pl.BlockSpec((planes, 24, LANES), lambda i: (0, 0, 0))
    high = lambda planes: pl.BlockSpec((planes, 24, LANES), lambda i: (0, ROWS // 24 - 1, 0))
    rows_a, rows_b = pl.pallas_call(
        outer_rows,
        grid=(1,),
        in_specs=[low(PLANES), low(PACKS), low(PACKS), high(PLANES), high(PACKS), high(PACKS)],
        out_specs=(whole(SENT * HALO, LANES), whole(888, LANES)),
        out_shape=(
            jax.ShapeDtypeStruct((SENT * HALO, LANES), f32),
            jax.ShapeDtypeStruct((888, LANES), f32),
        ),
        compiler_params=params,
    )(own, east_a, east_b, own, east_a, east_b)
    lat_first, lat_second = lat_swaps()
    north_b = lax.ppermute(rows_b, ("lon", "lat"), lat_second)
    north_a = lax.ppermute(rows_a, ("lon", "lat"), lat_first)

    turn_centre, turn_face = turning(lax.axis_index("lat"))
    levels, pair, single = (LEVELS, 2, TALL, LANES), (2, 2, TALL, LANES), (2, TALL, LANES)
    four, three = (4, 2, TALL, LANES), (3, 2, TALL, LANES)
    shapes = [levels] * 7 + [four, four, single, single, pair, single, three]
    done = pl.pallas_call(
        inner_rows,
        out_shape=tuple(jax.ShapeDtypeStruct(shape, f32) for shape in shapes),
        scratch_shapes=[pltpu.VMEM((16, 2, TALL, LANES), f32)]
        + [pltpu.VMEM(pair, f32), pltpu.VMEM(pair, f32), pltpu.VMEM(single, f32)],
        compiler_params=pltpu.CompilerParams(vmem_limit_bytes=12 * 1024 * 1024),
        cost_estimate=pl.CostEstimate(flops=40000000, bytes_accessed=12000000, transcendentals=0),
    )(own, east_a, east_b, north_a, turn_centre, turn_face)
    return pl.pallas_call(
        ocean_steps,
        out_shape=(
            jax.ShapeDtypeStruct(level_block, f32),
            jax.ShapeDtypeStruct(level_block, f32),
            jax.ShapeDtypeStruct((ROWS, LANES), f32),
        ),
        scratch_shapes=[pltpu.VMEM(levels, f32)] * 5
        + [pltpu.VMEM((16, 2, TALL, LANES), f32)]
        + [pltpu.VMEM(pair, f32), pltpu.VMEM(pair, f32), pltpu.VMEM(single, f32)],
        compiler_params=params,
    )(north_b, turn_centre, turn_face, *done)


def solution(mesh):
    return jax.shard_map(
        shards,
        mesh=mesh,
        in_specs=(
            P(None, "lat", "lon"),
            P(None, "lat", "lon"),
            P(None, "lat", "lon"),
            P("lat", "lon"),
            P(None, "lat", "lon"),
            P("lat", "lon"),
        ),
        out_specs=(P(None, "lat", "lon"), P(None, "lat", "lon"), P("lat", "lon")),
        check_vma=False,
    )
```

```python
import math

import jax
import jax.numpy as jnp
from jax import lax
from jax.experimental import pallas as pl
from jax.experimental.pallas import tpu as pltpu
from jax.sharding import PartitionSpec as P

SUBSTEPS = 8
STEPS = 2
LEVELS = 12
ROWS = 96
LANES = 128
HALO = 16
FOLD = 18

PLANES = 3 * LEVELS + 3
BOTTOM, FIRST, SURFACE = 36, 37, 38
PACKS = -(-PLANES // 8)
SENT = PLANES + 2 * PACKS

PAD = 8
EXT = 136
TALL = PAD + EXT + PAD
OWN = HALO
GHOST_A, PATCH, GHOST_B = OWN + ROWS, OWN + ROWS + 1, OWN + ROWS + 1 + FOLD
CHUNKS = ((0, 32), (32, 32), (64, 32), (96, 40))

viscosity = 0.05
friction = 0.1
coriolis = 0.25
substep_time = 0.4
layer = 1.0 / LEVELS
step_time = SUBSTEPS * substep_time
drag = 1.0 / (1.0 + step_time * friction)

VMEM_LIMIT = 24 * 1024 * 1024


def lanes_of(shape):
    return lax.broadcasted_iota(jnp.int32, shape, len(shape) - 1)


def masked_planes(u_ref, v_ref, d_ref, s_ref, m_ref, b_ref, ready):
    lane = lanes_of((ROWS, LANES))
    row = lax.broadcasted_iota(jnp.int32, (ROWS, LANES), 0)
    ready(5)
    ready(4)
    bottom = b_ref[...].astype(jnp.float32)
    first = bottom - jnp.sum(m_ref[...], axis=0).astype(jnp.float32)
    east = jnp.where(lane == LANES - 1, 12.0, pltpu.roll(bottom, LANES - 1, 1))
    north = jnp.where(row == ROWS - 1, 12.0, pltpu.roll(bottom, ROWS - 1, 0))
    up_u, up_v = jnp.minimum(bottom, east), jnp.minimum(bottom, north)
    ready(0)
    for k in range(LEVELS):
        yield k, jnp.where((first <= k) & (up_u > k), u_ref[k], 0.0)
    ready(1)
    for k in range(LEVELS):
        yield LEVELS + k, jnp.where((first <= k) & (up_v > k), v_ref[k], 0.0)
    ready(2)
    running = jnp.zeros_like(bottom)
    for k in range(LEVELS):
        weighted = jnp.where((first <= k) & (bottom > k), d_ref[k], 0.0)
        running = running + weighted
        yield 2 * LEVELS + k, layer * (running - 0.5 * weighted)
    ready(3)
    yield BOTTOM, bottom
    yield FIRST, first
    yield SURFACE, jnp.where(bottom > 0.0, s_ref[...], 0.0)


def strips(u_far, v_far, d_far, s_far, m_far, b_far, a_ref, c_ref, u_ref, v_ref, d_ref, s_ref, m_ref, b_ref, sems):
    pairs = ((u_far, u_ref), (v_far, v_ref), (d_far, d_ref), (s_far, s_ref), (m_far, m_ref), (b_far, b_ref))
    copies = [pltpu.make_async_copy(far, near, sems.at[i]) for i, (far, near) in enumerate(pairs)]
    for i in (5, 4, 0, 1, 2, 3):
        copies[i].start()
    lane = lanes_of((ROWS, LANES))
    even = lax.rem(lax.axis_index("lon"), 2) == 0
    for p, plane in masked_planes(u_ref, v_ref, d_ref, s_ref, m_ref, b_ref, lambda i: copies[i].wait()):
        slot = p % 8
        here = (lane >= HALO * slot) & (lane < HALO * slot + HALO)
        if slot == 0:
            to_east = to_west = jnp.zeros((ROWS, LANES), jnp.float32)
        to_east = jnp.where(here, pltpu.roll(plane, (HALO * slot + HALO) % LANES, 1), to_east)
        to_west = jnp.where(here, pltpu.roll(plane, HALO * slot, 1) if slot else plane, to_west)
        if slot == 7 or p == PLANES - 1:
            a_ref[p // 8] = jnp.where(even, to_east, to_west)
            c_ref[p // 8] = jnp.where(even, to_west, to_east)


def own_block(u_ref, v_ref, d_ref, s_ref, m_ref, b_ref, own_ref):
    for p, plane in masked_planes(u_ref, v_ref, d_ref, s_ref, m_ref, b_ref, lambda i: None):
        own_ref[p] = plane


def outer_rows(own_ref, ea_ref, eb_ref, a_ref, c_ref):
    even = lax.rem(lax.axis_index("lat"), 2) == 0
    for p in range(SENT):
        if p < PLANES:
            ref, at = own_ref, p
        elif p < PLANES + PACKS:
            ref, at = ea_ref, p - PLANES
        else:
            ref, at = eb_ref, p - PLANES - PACKS
        low, top = ref[at, pl.ds(0, 24), :], ref[at, pl.ds(ROWS - 24, 24), :]
        a_ref[pl.ds(p * HALO, HALO), :] = jnp.where(even, top[24 - HALO :], low[:HALO])
        c_ref[pl.ds(p * FOLD, FOLD), :] = jnp.where(even, low[:FOLD], top[24 - FOLD :])


def eastward(t0, t1):
    lane = lanes_of(t0.shape)
    r0, r1 = pltpu.roll(t0, LANES - 1, t0.ndim - 1), pltpu.roll(t1, LANES - 1, t0.ndim - 1)
    edge = lane == LANES - 1
    return jnp.where(edge, r1, r0), jnp.where(edge, r0, r1)


def westward(t0, t1):
    lane = lanes_of(t0.shape)
    r0, r1 = pltpu.roll(t0, 1, t0.ndim - 1), pltpu.roll(t1, 1, t0.ndim - 1)
    edge = lane == 0
    return jnp.where(edge, r1, r0), jnp.where(edge, r0, r1)


def fold_ghosts(ref, top, sign=1.0):
    for t in range(2):
        for ghost, source in ((GHOST_A, PATCH + FOLD - 2), (GHOST_B, OWN + ROWS - 2)):
            kept = ref[t, pl.ds(PAD + ghost, 1), :]
            taken = ref[t, pl.ds(PAD + source, 1), :]
            ref[t, pl.ds(PAD + ghost, 1), :] = jnp.where(top, sign * taken, kept)


(BED, FROM, UP_U, LO_U, UP_V, C_U, F_U, G_U, C_V, F_V, G_V, SUM_U, SUM_V, NEW_U, NEW_V, SEA) = range(16)
INNER = (3, 12)
CORE = (4, 11)
CORE_ROWS = 88
SUMS = (G_U, G_V, NEW_U, NEW_V)


def beyond(p):
    return 12.0 if p in (BOTTOM, FIRST) else 0.0


def beside(east, west, p):
    lane = lanes_of(east.shape)
    slot = HALO * (p % 8)
    e = pltpu.roll(east, LANES - slot, 1) if slot else east
    w = pltpu.roll(west, (2 * LANES - HALO - slot) % LANES, 1) if slot != LANES - HALO else west
    return jnp.where(lane < HALO, e, jnp.where(lane >= LANES - HALO, w, beyond(p)))


def planes_of(pack):
    return range(8 * pack, min(8 * pack + 8, PLANES))


def faces(at, n, flat, ft_ref, fv_ref, top):
    rows, up = pl.ds(PAD + at, n), pl.ds(PAD + at + 1, n)
    bed = [flat[BED, t, rows, :] for t in range(2)]
    start = [flat[FROM, t, rows, :] for t in range(2)]
    bed_east = eastward(*bed)
    start_east = eastward(*start)
    ext_row = lax.broadcasted_iota(jnp.int32, (n, LANES), 0) + at
    mirror = (ext_row >= jnp.where(top, PATCH, EXT)) & (ext_row < PATCH + FOLD)
    for t in range(2):
        up_u = jnp.minimum(bed[t], bed_east[t])
        lo_u = jnp.where(mirror, start_east[t], start[t])
        up_v = jnp.minimum(bed[t], flat[BED, t, up, :])
        count_u = jnp.maximum(up_u - lo_u, 0.0)
        count_v = jnp.maximum(up_v - start[t], 0.0)
        flat[UP_U, t, rows, :] = up_u
        flat[LO_U, t, rows, :] = lo_u
        flat[UP_V, t, rows, :] = up_v
        flat[C_U, t, rows, :] = count_u * (-substep_time * layer)
        flat[C_V, t, rows, :] = count_v * (-substep_time * layer)
        flat[F_U, t, rows, :] = jnp.where(count_u > 0.0, substep_time * ft_ref[rows, :], 0.0)
        flat[F_V, t, rows, :] = jnp.where(count_v > 0.0, -substep_time * fv_ref[rows, :], 0.0)
        flat[SEA, t, rows, :] = jnp.where(bed[t] > 0.0, substep_time, 0.0)


def mask_rows(r, flat, u_all, v_all, flow_u, flow_v):
    rows = pl.ds(pl.multiple_of(r * 8, 8) + PAD, 8)
    for t in range(2):
        lo_u, up_u = flat[LO_U, t, rows, :], flat[UP_U, t, rows, :]
        lo_v, up_v = flat[FROM, t, rows, :], flat[UP_V, t, rows, :]
        us = [jnp.where((lo_u <= k) & (up_u > k), u_all[k, t, rows, :], 0.0) for k in range(LEVELS)]
        vs = [jnp.where((lo_v <= k) & (up_v > k), v_all[k, t, rows, :], 0.0) for k in range(LEVELS)]
        for k in range(LEVELS):
            u_all[k, t, rows, :] = us[k]
            v_all[k, t, rows, :] = vs[k]
        flow_u[0, t, rows, :] = layer * sum(us[1:], us[0])
        flow_v[0, t, rows, :] = layer * sum(vs[1:], vs[0])


def tendencies(r, flat, ft_ref, fv_ref, u_all, v_all, p_all, u_new, v_new):
    base = pl.multiple_of(r * 8, 8) + PAD
    rows, up, down = pl.ds(base, 8), pl.ds(base + 1, 8), pl.ds(base - 1, 8)
    ft, fv = ft_ref[rows, :], fv_ref[rows, :]
    lo_u = [flat[LO_U, t, rows, :] for t in range(2)]
    up_u = [flat[UP_U, t, rows, :] for t in range(2)]
    lo_v = [flat[FROM, t, rows, :] for t in range(2)]
    up_v = [flat[UP_V, t, rows, :] for t in range(2)]
    zero = jnp.zeros((8, LANES), jnp.float32)
    force_u, force_v, total_u, total_v = [zero] * 2, [zero] * 2, [zero] * 2, [zero] * 2
    for k in range(LEVELS):
        eu, wu, ru, ev, wv, rv, u0s, v0s = [], [], [], [], [], [], [], []
        for t in range(2):
            u0, un, us = u_all[k, t, rows, :], u_all[k, t, up, :], u_all[k, t, down, :]
            v0, vn, vs = v_all[k, t, rows, :], v_all[k, t, up, :], v_all[k, t, down, :]
            p0, pn = p_all[k, t, rows, :], p_all[k, t, up, :]
            turn_v = ft * (v0 + vs)
            turn_u = fv * (u0 + un)
            a = viscosity * u0
            c = viscosity * v0
            eu.append(a - p0 + turn_v)
            wu.append(a)
            ru.append(viscosity * (un + us) - 4.0 * a + p0 + turn_v)
            ev.append(c)
            wv.append(c - turn_u)
            rv.append(viscosity * (vn + vs) - 4.0 * c + (p0 - pn) - turn_u)
            u0s.append(u0)
            v0s.append(v0)
        eu, wu, ev, wv = eastward(*eu), westward(*wu), eastward(*ev), westward(*wv)
        for t in range(2):
            tend_u = jnp.where((lo_u[t] <= k) & (up_u[t] > k), eu[t] + wu[t] + ru[t], 0.0)
            tend_v = jnp.where((lo_v[t] <= k) & (up_v[t] > k), ev[t] + wv[t] + rv[t], 0.0)
            force_u[t] = force_u[t] + tend_u
            force_v[t] = force_v[t] + tend_v
            new_u = u0s[t] + step_time * tend_u
            new_v = v0s[t] + step_time * tend_v
            new_u = jnp.where(up_u[t] == k + 1, drag * new_u, new_u)
            new_v = jnp.where(up_v[t] == k + 1, drag * new_v, new_v)
            total_u[t] = total_u[t] + new_u
            total_v[t] = total_v[t] + new_v
            u_new[k, t, rows, :] = new_u
            v_new[k, t, rows, :] = new_v
    for t in range(2):
        flat[G_U, t, rows, :] = (substep_time * layer) * force_u[t]
        flat[G_V, t, rows, :] = (substep_time * layer) * force_v[t]
        flat[NEW_U, t, rows, :] = layer * total_u[t]
        flat[NEW_V, t, rows, :] = layer * total_v[t]


def substep(now, later, chunks, top, flat, flow_u, flow_v, height):
    for at, n in chunks:
        rows, down = pl.ds(PAD + at, n), pl.ds(PAD + at - 1, n)
        u = [flow_u[now, t, rows, :] for t in range(2)]
        uw = westward(*u)
        for t in range(2):
            spread = u[t] - uw[t] + flow_v[now, t, rows, :] - flow_v[now, t, down, :]
            height[t, rows, :] = height[t, rows, :] - flat[SEA, t, rows, :] * spread
    if top is not None:
        fold_ghosts(height, top)
    for at, n in chunks:
        rows, up, down = pl.ds(PAD + at, n), pl.ds(PAD + at + 1, n), pl.ds(PAD + at - 1, n)
        h = [height[t, rows, :] for t in range(2)]
        he = eastward(*h)
        qv = [flow_v[now, t, rows, :] + flow_v[now, t, down, :] for t in range(2)]
        qve = eastward(*qv)
        qu = [flow_u[now, t, rows, :] + flow_u[now, t, up, :] for t in range(2)]
        quw = westward(*qu)
        for t in range(2):
            next_u = (
                flow_u[now, t, rows, :]
                + flat[C_U, t, rows, :] * (he[t] - h[t])
                + flat[F_U, t, rows, :] * (qv[t] + qve[t])
                + flat[G_U, t, rows, :]
            )
            next_v = (
                flow_v[now, t, rows, :]
                + flat[C_V, t, rows, :] * (height[t, up, :] - h[t])
                + flat[F_V, t, rows, :] * (qu[t] + quw[t])
                + flat[G_V, t, rows, :]
            )
            flow_u[later, t, rows, :] = next_u
            flow_v[later, t, rows, :] = next_v
            flat[SUM_U, t, rows, :] = flat[SUM_U, t, rows, :] + next_u
            flat[SUM_V, t, rows, :] = flat[SUM_V, t, rows, :] + next_v
    if top is not None:
        fold_ghosts(flow_u.at[later], top)


def substeps(chunks, top, flat, flow_u, flow_v, height):
    for which in (SUM_U, SUM_V):
        for t in range(2):
            flat[which, t, pl.ds(PAD, EXT), :] = jnp.zeros((EXT, LANES), jnp.float32)

    def two(turn, carry):
        substep(0, 1, chunks, top, flat, flow_u, flow_v, height)
        substep(1, 0, chunks, top, flat, flow_u, flow_v, height)
        return carry

    lax.fori_loop(0, SUBSTEPS // 2, two, 0)


def correct(first, end, flat, u_from, v_from, u_to, v_to, flow_u, flow_v):
    def tile(r, carry):
        rows = pl.ds(pl.multiple_of(r * 8, 8) + PAD, 8)
        last = flow_u is None
        for t in range(1 if last else 2):
            lo_u, up_u = flat[LO_U, t, rows, :], flat[UP_U, t, rows, :]
            lo_v, up_v = flat[FROM, t, rows, :], flat[UP_V, t, rows, :]
            mean_u = flat[SUM_U, t, rows, :] / SUBSTEPS
            mean_v = flat[SUM_V, t, rows, :] / SUBSTEPS
            depth_u = layer * jnp.maximum(up_u - lo_u, 1.0)
            depth_v = layer * jnp.maximum(up_v - lo_v, 1.0)
            add_u = (mean_u - flat[NEW_U, t, rows, :]) / depth_u
            add_v = (mean_v - flat[NEW_V, t, rows, :]) / depth_v
            us = [jnp.where((lo_u <= k) & (up_u > k), u_from[k, t, rows, :] + add_u, 0.0) for k in range(LEVELS)]
            vs = [jnp.where((lo_v <= k) & (up_v > k), v_from[k, t, rows, :] + add_v, 0.0) for k in range(LEVELS)]
            for k in range(LEVELS):
                if last:
                    out = pl.ds(pl.multiple_of(r * 8 - OWN, 8), 8)
                    u_to[k, out, :] = us[k]
                    v_to[k, out, :] = vs[k]
                else:
                    u_to[k, t, rows, :] = us[k]
                    v_to[k, t, rows, :] = vs[k]
            if not last:
                flow_u[0, t, rows, :] = mean_u
                flow_v[0, t, rows, :] = mean_v
        return carry

    lax.fori_loop(first, end, tile, 0)


def inner_rows(
    own_ref, ea_ref, eb_ref, na_ref, ft_ref, fv_ref,
    u_all, v_all, p_all, u_new, v_new, u_next, v_next, sums, later_sums, bed, start, flows, height_in, later,
    flat, flow_u, flow_v, height,
):
    even_lat = lax.rem(lax.axis_index("lat"), 2) == 0
    even_lon = lax.rem(lax.axis_index("lon"), 2) == 0
    place = [u_all.at[k] for k in range(LEVELS)] + [v_all.at[k] for k in range(LEVELS)]
    place += [p_all.at[k] for k in range(LEVELS)] + [flat.at[BED], flat.at[FROM], height]
    for pack in range(PACKS):
        for at in range(0, ROWS, 32):
            a, b = ea_ref[pack, pl.ds(at, 32), :], eb_ref[pack, pl.ds(at, 32), :]
            east, west = jnp.where(even_lon, a, b), jnp.where(even_lon, b, a)
            tiles = [beside(east, west, p) for p in planes_of(pack)]
            for p, tile in zip(planes_of(pack), tiles):
                place[p][0, pl.ds(PAD + OWN + at, 32), :] = own_ref[p, pl.ds(at, 32), :]
                place[p][1, pl.ds(PAD + OWN + at, 32), :] = tile
        at = pl.multiple_of(jnp.where(even_lat, PAD + OWN + ROWS, PAD), 8)
        a, b = na_ref[pl.ds((PLANES + pack) * HALO, HALO), :], na_ref[pl.ds((PLANES + PACKS + pack) * HALO, HALO), :]
        east, west = jnp.where(even_lon, a, b), jnp.where(even_lon, b, a)
        tiles = [(na_ref[pl.ds(p * HALO, HALO), :], beside(east, west, p)) for p in planes_of(pack)]
        for p, (t0, t1) in zip(planes_of(pack), tiles):
            place[p][0, pl.ds(at, HALO), :] = t0
            place[p][1, pl.ds(at, HALO), :] = t1
            for t in range(2):
                place[p][t, pl.ds(0, PAD), :] = jnp.full((PAD, LANES), beyond(p), jnp.float32)
                place[p][t, pl.ds(TALL - 16, 16), :] = jnp.full((16, LANES), beyond(p), jnp.float32)
    for at, n in CHUNKS:
        faces(at, n, flat, ft_ref, fv_ref, False)
    for t in range(2):
        for flow in (flow_u, flow_v):
            for now in range(2):
                flow[now, t, :, :] = jnp.zeros((TALL, LANES), jnp.float32)
        for which in (G_U, G_V):
            flat[which, t, pl.ds(PAD, EXT), :] = jnp.zeros((EXT, LANES), jnp.float32)

    def first(r, carry):
        mask_rows(r, flat, u_all, v_all, flow_u, flow_v)
        return carry

    def second(r, carry):
        tendencies(r, flat, ft_ref, fv_ref, u_all, v_all, p_all, u_new, v_new)
        return carry

    tiles = EXT // 8
    lax.fori_loop(jnp.where(even_lat, INNER[0] - 1, 0), jnp.where(even_lat, tiles, INNER[1] + 1), first, 0)
    begin, end = jnp.where(even_lat, INNER[0], 0), jnp.where(even_lat, tiles - 1, INNER[1])
    lax.fori_loop(begin, end, second, 0)
    own = pl.ds(PAD + OWN, ROWS)
    inner = pl.ds(PAD + 8 * INNER[0], 8 * (INNER[1] - INNER[0]))
    masked = pl.ds(PAD + 8 * (INNER[0] - 1), 8 * (INNER[1] - INNER[0] + 2))
    core = pl.ds(pl.multiple_of(jnp.where(even_lat, PAD + 8 * CORE[0], PAD), 8), CORE_ROWS)
    for t in range(2):
        bed[t, :, :] = flat[BED, t, :, :]
        start[t, :, :] = flat[FROM, t, :, :]
        height_in[t, own, :] = height[t, own, :]
        flows[0, t, masked, :] = flow_u[0, t, masked, :]
        flows[1, t, masked, :] = flow_v[0, t, masked, :]
        for i, which in enumerate(SUMS):
            sums[i, t, inner, :] = flat[which, t, inner, :]
    base = pl.multiple_of(8 * begin, 8)
    substeps(((base, 32), (base + 32, 32), (base + 64, 40)), None, flat, flow_u, flow_v, height)
    correct(begin, end, flat, u_new, v_new, u_next, v_next, flow_u, flow_v)

    def third(r, carry):
        tendencies(r, flat, ft_ref, fv_ref, u_next, v_next, p_all, u_new, v_new)
        return carry

    lax.fori_loop(jnp.where(even_lat, CORE[0], 1), jnp.where(even_lat, tiles - 2, CORE[1]), third, 0)
    for t in range(2):
        later[0, t, core, :] = flow_u[0, t, core, :]
        later[1, t, core, :] = flow_v[0, t, core, :]
        later[2, t, core, :] = height[t, core, :]
        for i, which in enumerate(SUMS):
            later_sums[i, t, core, :] = flat[which, t, core, :]


def ocean_steps(
    nb_ref, ft_ref, fv_ref,
    u_in, v_in, p_in, u_done, v_done, u_next, v_next, sums, later_sums, bed, start, flows, height_in, later,
    u_out, v_out, h_out,
    u_all, v_all, p_all, u_new, v_new,
    flat, flow_u, flow_v, height,
):
    lat = lax.axis_index("lat")
    even_lat = lax.rem(lat, 2) == 0
    even_lon = lax.rem(lax.axis_index("lon"), 2) == 0
    top = lat == lax.axis_size("lat") - 1
    place = [u_all.at[k] for k in range(LEVELS)] + [v_all.at[k] for k in range(LEVELS)]
    place += [p_all.at[k] for k in range(LEVELS)] + [flat.at[BED], flat.at[FROM], height]

    own = pl.ds(PAD + OWN, ROWS)
    low = pl.ds(PAD + OWN, 8 * (CORE[0] + 1) - OWN)
    high = pl.ds(PAD + 8 * (CORE[1] - 1), OWN + ROWS - 8 * (CORE[1] - 1))
    core = pl.ds(pl.multiple_of(jnp.where(even_lat, PAD + 8 * CORE[0], PAD), 8), CORE_ROWS)
    inner = pl.ds(PAD + 8 * INNER[0], 8 * (INNER[1] - INNER[0]))
    masked = pl.ds(PAD + 8 * (INNER[0] - 1), 8 * (INNER[1] - INNER[0] + 2))
    for t in range(2):
        for k in range(LEVELS):
            for rows in (low, high):
                p_all[k, t, rows, :] = p_in[k, t, rows, :]
                u_all[k, t, rows, :] = u_in[k, t, rows, :]
                v_all[k, t, rows, :] = v_in[k, t, rows, :]
        flat[BED, t, :, :] = bed[t, :, :]
        flat[FROM, t, :, :] = start[t, :, :]
        for flow in (flow_u, flow_v):
            for now in range(2):
                flow[now, t, :, :] = jnp.zeros((TALL, LANES), jnp.float32)
        height[t, own, :] = height_in[t, own, :]
        flow_u[0, t, masked, :] = flows[0, t, masked, :]
        flow_v[0, t, masked, :] = flows[1, t, masked, :]
        for i, which in enumerate(SUMS):
            flat[which, t, inner, :] = sums[i, t, inner, :]
            flat[which, t, pl.ds(PAD + EXT - 8, 8), :] = jnp.zeros((8, LANES), jnp.float32)

    edge, after = pl.ds(0, PAD), pl.ds(PAD + OWN + ROWS + HALO, 16)
    at = pl.multiple_of(jnp.where(even_lat, PAD, PAD + OWN + ROWS), 8)

    def rows_of(p):
        return jnp.where(even_lat, nb_ref[pl.ds(p * FOLD + FOLD - HALO, HALO), :], nb_ref[pl.ds(p * FOLD, HALO), :])

    for pack in range(PACKS):
        a, b = rows_of(PLANES + pack), rows_of(PLANES + PACKS + pack)
        east, west = jnp.where(even_lon, a, b), jnp.where(even_lon, b, a)
        tiles = [(rows_of(p), beside(east, west, p)) for p in planes_of(pack)]
        for p, (t0, t1) in zip(planes_of(pack), tiles):
            place[p][0, pl.ds(at, HALO), :] = t0
            place[p][1, pl.ds(at, HALO), :] = t1
        for p in planes_of(pack):
            for t in range(2):
                place[p][t, edge, :] = jnp.full((PAD, LANES), beyond(p), jnp.float32)
                place[p][t, after, :] = jnp.full((16, LANES), beyond(p), jnp.float32)

    @pl.when(top)
    def _():
        lane = lanes_of((24, LANES))

        def flipped(x):
            return jnp.take_along_axis(x, LANES - 1 - lane, axis=1)

        for pack in range(PACKS):
            a = flipped(nb_ref[pl.ds((PLANES + pack) * FOLD, 24), :])
            b = flipped(nb_ref[pl.ds((PLANES + PACKS + pack) * FOLD, 24), :])
            east, west = jnp.where(even_lon, b, a), jnp.where(even_lon, a, b)
            tiles = []
            for p in planes_of(pack):
                slot = HALO * (p % 8)
                e = pltpu.roll(west, (slot + HALO) % LANES, 1) if slot != LANES - HALO else west
                w = pltpu.roll(east, slot, 1) if slot else east
                t0 = flipped(nb_ref[pl.ds(p * FOLD, 24), :])
                t1 = jnp.where(lane < HALO, e, jnp.where(lane >= LANES - HALO, w, beyond(p)))
                if p < LEVELS:
                    t0, t1 = eastward(t0, t1)
                    t0, t1 = -t0, -t1
                tiles.append((t0, t1))
            for p, (t0, t1) in zip(planes_of(pack), tiles):
                place[p][0, pl.ds(PAD + PATCH, FOLD), :] = t0[:FOLD]
                place[p][1, pl.ds(PAD + PATCH, FOLD), :] = t1[:FOLD]

    fold_ghosts(flat.at[BED], top)
    for at, n in CHUNKS:
        faces(at, n, flat, ft_ref, fv_ref, top)
    def mask_first(r, carry):
        mask_rows(r, flat, u_all, v_all, flow_u, flow_v)
        return carry

    tiles = EXT // 8
    lax.fori_loop(jnp.where(even_lat, 0, INNER[1] + 1), jnp.where(even_lat, INNER[0] - 1, tiles), mask_first, 0)

    def ghosts():
        for k in range(LEVELS):
            fold_ghosts(u_all.at[k], top)
            fold_ghosts(v_all.at[k], top, -1.0)
        fold_ghosts(flow_u.at[0], top)

    def tend(r, carry):
        tendencies(r, flat, ft_ref, fv_ref, u_all, v_all, p_all, u_new, v_new)
        return carry

    for k in range(LEVELS):
        fold_ghosts(p_all.at[k], top)
    ghosts()
    first, end = jnp.where(even_lat, 0, INNER[1]), jnp.where(even_lat, INNER[0], jnp.where(top, tiles, tiles - 1))
    lax.fori_loop(first, end, tend, 0)
    base = pl.multiple_of(jnp.where(even_lat, 0, 8 * CORE[1] - 8), 8)
    substeps(((base, 24), (base + 24, 32)), top, flat, flow_u, flow_v, height)
    correct(first, jnp.where(even_lat, INNER[0], tiles), flat, u_new, v_new, u_all, v_all, flow_u, flow_v)
    between = jnp.where(even_lat, INNER[0], CORE[1])
    correct(between, between + 1, flat, u_done, v_done, u_all, v_all, flow_u, flow_v)

    for t in range(2):
        for k in range(LEVELS):
            for at in (8 * CORE[0], 8 * CORE[1] - 8):
                rows = pl.ds(PAD + at, 8)
                u_all[k, t, rows, :] = u_next[k, t, rows, :]
                v_all[k, t, rows, :] = v_next[k, t, rows, :]
        flow_u[0, t, core, :] = later[0, t, core, :]
        flow_v[0, t, core, :] = later[1, t, core, :]
        height[t, core, :] = later[2, t, core, :]
        for i, which in enumerate(SUMS):
            flat[which, t, core, :] = later_sums[i, t, core, :]
    ghosts()
    end = jnp.where(even_lat, CORE[0], jnp.where(top, tiles, tiles - 2))
    lax.fori_loop(jnp.where(even_lat, 1, CORE[1]), end, tend, 0)
    substeps(((8, 40), (48, 40), (88, 48)), top, flat, flow_u, flow_v, height)
    low, high = OWN // 8, (OWN + ROWS) // 8
    here = jnp.where(even_lat, low, CORE[1]), jnp.where(even_lat, CORE[0], high)
    done = jnp.where(even_lat, CORE[0], low), jnp.where(even_lat, high, CORE[1])
    correct(*here, flat, u_new, v_new, u_out, v_out, None, None)
    correct(*done, flat, u_done, v_done, u_out, v_out, None, None)
    h_out[...] = height[0, pl.ds(PAD + OWN, ROWS), :]


def lon_swaps():
    count = lax.axis_size("lon")
    first = [(i, i ^ 1) for i in range(count)]
    second = [(i, (((i + 1) % count) ^ 1) - 1) for i in range(count)]
    return first, [(i, j % count) for i, j in second]


def lat_swaps():
    lats, lons = lax.axis_size("lat"), lax.axis_size("lon")
    first, second = [], []
    for lat in range(lats):
        for lon in range(lons):
            first.append((lon * lats + lat, lon * lats + (lat ^ 1)))
            if lat == lats - 1:
                second.append((lon * lats + lat, (lons - 1 - lon) * lats + lat))
            elif lat:
                second.append((lon * lats + lat, lon * lats + ((lat + 1) ^ 1) - 1))
    return first, second


def turning(lat):
    lats = lax.axis_size("lat")
    ext = jnp.arange(TALL, dtype=jnp.int32) - PAD
    mirror = (lat == lats - 1) & (ext >= PATCH)
    row = jnp.where(mirror, lats * ROWS - FOLD + ext - PATCH, lat * ROWS + ext - OWN).astype(jnp.float32)
    sign = jnp.where(mirror, -0.25 * coriolis, 0.25 * coriolis)
    cells = lats * ROWS
    centre = sign * jnp.sin(math.pi * ((row + 0.5) / cells - 0.5))
    face = sign * jnp.sin(math.pi * ((row + 1.0) / cells - 0.5))
    wide = (TALL, LANES)
    return jnp.broadcast_to(centre[:, None], wide), jnp.broadcast_to(face[:, None], wide)


def shards(u_velocity, v_velocity, density, surface, land_mask, bottom):
    f32 = jnp.float32
    params = pltpu.CompilerParams(vmem_limit_bytes=VMEM_LIMIT)
    level_block = (LEVELS, ROWS, LANES)
    fields = (u_velocity, v_velocity, density, surface, land_mask, bottom)
    pack_a, pack_b = pl.pallas_call(
        strips,
        out_shape=(jax.ShapeDtypeStruct((PACKS, ROWS, LANES), f32),) * 2,
        in_specs=[pl.BlockSpec(memory_space=pltpu.HBM)] * 6,
        scratch_shapes=[pltpu.VMEM(level_block, f32)] * 3
        + [pltpu.VMEM((ROWS, LANES), f32), pltpu.VMEM(level_block, jnp.int32), pltpu.VMEM((ROWS, LANES), jnp.int32)]
        + [pltpu.SemaphoreType.DMA((6,))],
        compiler_params=pltpu.CompilerParams(vmem_limit_bytes=56 * 1024 * 1024),
    )(*fields)
    lon_first, lon_second = lon_swaps()
    east_a = lax.ppermute(pack_a, "lon", lon_first)
    east_b = lax.ppermute(pack_b, "lon", lon_second)
    own = pl.pallas_call(
        own_block,
        out_shape=jax.ShapeDtypeStruct((PLANES, ROWS, LANES), f32),
        compiler_params=pltpu.CompilerParams(vmem_limit_bytes=8 * 1024 * 1024),
        cost_estimate=pl.CostEstimate(flops=4000000, bytes_accessed=5000000, transcendentals=0),
    )(*fields)

    rows_a, rows_b = pl.pallas_call(
        outer_rows,
        out_shape=(
            jax.ShapeDtypeStruct((SENT * HALO, LANES), f32),
            jax.ShapeDtypeStruct((888, LANES), f32),
        ),
        compiler_params=pltpu.CompilerParams(vmem_limit_bytes=8 * 1024 * 1024),
    )(own, east_a, east_b)
    lat_first, lat_second = lat_swaps()
    north_b = lax.ppermute(rows_b, ("lon", "lat"), lat_second)
    north_a = lax.ppermute(rows_a, ("lon", "lat"), lat_first)

    turn_centre, turn_face = turning(lax.axis_index("lat"))
    levels, pair, single = (LEVELS, 2, TALL, LANES), (2, 2, TALL, LANES), (2, TALL, LANES)
    four, three = (4, 2, TALL, LANES), (3, 2, TALL, LANES)
    shapes = [levels] * 7 + [four, four, single, single, pair, single, three]
    done = pl.pallas_call(
        inner_rows,
        out_shape=tuple(jax.ShapeDtypeStruct(shape, f32) for shape in shapes),
        scratch_shapes=[pltpu.VMEM((16, 2, TALL, LANES), f32)]
        + [pltpu.VMEM(pair, f32), pltpu.VMEM(pair, f32), pltpu.VMEM(single, f32)],
        compiler_params=pltpu.CompilerParams(vmem_limit_bytes=12 * 1024 * 1024),
        cost_estimate=pl.CostEstimate(flops=40000000, bytes_accessed=12000000, transcendentals=0),
    )(own, east_a, east_b, north_a, turn_centre, turn_face)
    return pl.pallas_call(
        ocean_steps,
        out_shape=(
            jax.ShapeDtypeStruct(level_block, f32),
            jax.ShapeDtypeStruct(level_block, f32),
            jax.ShapeDtypeStruct((ROWS, LANES), f32),
        ),
        scratch_shapes=[pltpu.VMEM(levels, f32)] * 5
        + [pltpu.VMEM((16, 2, TALL, LANES), f32)]
        + [pltpu.VMEM(pair, f32), pltpu.VMEM(pair, f32), pltpu.VMEM(single, f32)],
        compiler_params=params,
    )(north_b, turn_centre, turn_face, *done)


def solution(mesh):
    return jax.shard_map(
        shards,
        mesh=mesh,
        in_specs=(
            P(None, "lat", "lon"),
            P(None, "lat", "lon"),
            P(None, "lat", "lon"),
            P("lat", "lon"),
            P(None, "lat", "lon"),
            P("lat", "lon"),
        ),
        out_specs=(P(None, "lat", "lon"), P(None, "lat", "lon"), P("lat", "lon")),
        check_vma=False,
    )
```
